512 devices in a mesh: leaf: 64 (over x, y, core), grid: 8 (over z).
Axes of the slice: x: 4, y: 8, z: 8, core: 2. Of those that a mesh axis runs over, the one named last changes fastest.
Arguments:
- right_side: float32 [7, 256, 4096], P(None, None, ('leaf', 'grid')), may hold values from -6 to 6
- diag_inv: float32 [4096, 8128], P('leaf'), as said below
- off_diag: float32 [21, 256, 4096], P(None, None, 'leaf'), may hold values from -0.09375 to 0.09375
- tile_rows: int32 [21, 2, 64], P(None, None, 'leaf'), may hold values from 0 to 31, as said below
Outputs:
- forward_solution: float32 [7, 256, 4096], P(None, None, ('leaf', 'grid'))
- solution: float32 [7, 256, 4096], P(None, None, ('leaf', 'grid'))
The draws below stay inside these ranges and needn't reach their ends.
Inputs may be any that keep to these rules, and one draw needn't show every extreme that they name: tile_rows[p, t, i] for the pair p of levels l < k names one of the 64 * 2^k / 128 tiles of 128 rows of the level-k separator above leaf index i. Within each separator's block of diag_inv, the diagonal entries lie near 0.8 to 1.2, and every row's other entries have a root mean square of about 0.5 divided by the square root of the separator's width.
All inputs are finite; a program needn't handle non-finite values.
Results may differ from the reference program's by a relative error of at most 0.0001.
Values sent between devices are 32-bit elements; how exact they have to be, the bound alone decides.
A program may use at most 64 MiB of HBM per device.

```python
import jax
import jax.numpy as jnp
from jax import lax

P_SIZE = 64
R = 256
TILE = 128
TILES = 2
LEVELS = 7
PAIRS = 21
ROWS = 4096
COLS = 8128
N_LEAF = 64


def draw_diag_inv(key, part):
    key = jax.random.fold_in(key, 11)
    noise_key, diag_key = jax.random.split(key)
    row_index = jnp.arange(ROWS, dtype=jnp.int32)[:, None]
    column = jnp.arange(COLS, dtype=jnp.int32)[None, :]
    node_width = jnp.full((1, COLS), P_SIZE, dtype=jnp.int32)
    node_start = jnp.zeros((1, COLS), dtype=jnp.int32)
    for height in range(1, LEVELS):
        inside = column >= P_SIZE * (2 ** height - 1)
        node_width = jnp.where(inside, P_SIZE * 2 ** height, node_width)
        node_start = jnp.where(inside, P_SIZE * (2 ** height - 1), node_start)
    on_diagonal = row_index % node_width == column - node_start
    noise = jax.random.normal(noise_key, (ROWS, COLS), jnp.float32)
    scale = 0.5 / jnp.sqrt(node_width.astype(jnp.float32))
    diagonal = jax.random.uniform(diag_key, (ROWS, COLS), jnp.float32, 0.8, 1.2)
    return noise * scale + jnp.where(on_diagonal, diagonal, 0.0)


def draw_tile_rows(key, part):
    key = jax.random.fold_in(key, 23)
    first_key, step_key = jax.random.split(key)
    counts = []
    for ancestor in range(1, LEVELS):
        for source in range(ancestor):
            counts.append(P_SIZE * 2 ** ancestor // TILE)
    tile_count = jnp.array(counts, dtype=jnp.int32)[:, None, None]
    first = jax.random.randint(first_key, (PAIRS, 1, N_LEAF), 0, tile_count, dtype=jnp.int32)
    leaf_ids = jnp.arange(N_LEAF, dtype=jnp.int32)[None, None, :]
    first = jnp.where(leaf_ids == 0, tile_count - 1, first)
    first = jnp.where(leaf_ids == 1, jnp.zeros_like(first), first)
    stride = jax.random.randint(step_key, (PAIRS, 1, N_LEAF), 0, jnp.maximum(tile_count - 1, 1), dtype=jnp.int32)
    steps_along = jnp.arange(TILES, dtype=jnp.int32)[None, :, None]
    return (first + steps_along * (1 + stride)) % tile_count


def block_scale(key, shape, shards, smallest, largest):
    gain, own = 1.0, jax.random.fold_in(key, 6)
    for axis_at, shards_of in shards:
        heights = jnp.exp(jax.random.uniform(jax.random.fold_in(own, axis_at), (shards_of,), jnp.float32, smallest / len(shards), largest / len(shards)))
        gain = gain * jnp.repeat(heights, shape[axis_at] // shards_of).reshape([-1 if axis == axis_at else 1 for axis in range(len(shape))])
    return gain


def bell_draw(key, dims, deviation, bound, cuts=(), kind=jnp.bfloat16):
    result = jax.random.normal(key, dims, jnp.float32) * deviation
    if len(cuts) > 0:
        result = block_scale(key, dims, cuts, -0.22, 0.18) * result
    return jnp.clip(result, min=-bound, max=bound).astype(kind)


def setup_inputs(seed: int = 0) -> dict:
    streams_of = jax.random.split(jax.random.key(seed), 5)
    right_side = bell_draw(streams_of[0], (LEVELS, R, ROWS), 1.0, 6.0, ((2, 512),), jnp.float32)
    diag_inv = draw_diag_inv(jax.random.fold_in(streams_of[4], 71), 0)
    off_diag = bell_draw(streams_of[2], (PAIRS, TILES * TILE, ROWS), (2 * TILES * TILE * LEVELS) ** -0.5, 0.09375, ((2, 64),), jnp.float32)
    tile_rows = draw_tile_rows(jax.random.fold_in(streams_of[4], 71), 0)
    return dict(right_side=right_side, diag_inv=diag_inv, off_diag=off_diag, tile_rows=tile_rows)


highest = lax.Precision.HIGHEST


def pair_slot(source, ancestor):
    return ancestor * (ancestor - 1) // 2 + source


def tile_targets(tile_rows, pair, height):
    node_width = P_SIZE * 2 ** height
    leaf_ids = jnp.arange(N_LEAF, dtype=jnp.int32)
    node_start = (leaf_ids // (2 ** height)) * node_width
    tile_base = node_start[:, None] + tile_rows[pair].T.astype(jnp.int32) * TILE
    return tile_base[:, :, None] + jnp.arange(TILE, dtype=jnp.int32)[None, None, :]


def blocks_of(diag_inv, height):
    node_width = P_SIZE * 2 ** height
    offset = P_SIZE * (2 ** height - 1)
    return diag_inv[:, offset:offset + node_width].reshape(ROWS // node_width, node_width, node_width)


def reference(right_side, diag_inv, off_diag, tile_rows):
    forward = []
    for height in range(LEVELS):
        update = jnp.zeros((R, ROWS), jnp.float32)
        for source in range(height):
            pair = pair_slot(source, height)
            values = off_diag[pair].reshape(TILES, TILE, N_LEAF, P_SIZE)
            known_part = forward[source].reshape(R, N_LEAF, P_SIZE)
            addend = jnp.einsum('stnp,rnp->rnst', values, known_part, precision=highest)
            targets = tile_targets(tile_rows, pair, height)
            update = update.at[:, targets].add(addend)
        node_width = P_SIZE * 2 ** height
        blocks = blocks_of(diag_inv, height)
        reduced = (right_side[height] - update).reshape(R, ROWS // node_width, node_width)
        forward.append(jnp.einsum('jab,rjb->rja', blocks, reduced, precision=highest).reshape(R, ROWS))
    backward = [None] * LEVELS
    for height in reversed(range(LEVELS)):
        known_sum = jnp.zeros((R, N_LEAF, P_SIZE), jnp.float32)
        for ancestor in range(height + 1, LEVELS):
            pair = pair_slot(height, ancestor)
            values = off_diag[pair].reshape(TILES, TILE, N_LEAF, P_SIZE)
            targets = tile_targets(tile_rows, pair, ancestor)
            picked = backward[ancestor][:, targets]
            known_sum = known_sum + jnp.einsum('stnp,rnst->rnp', values, picked, precision=highest)
        node_width = P_SIZE * 2 ** height
        blocks = blocks_of(diag_inv, height)
        residue = (forward[height] - known_sum.reshape(R, ROWS)).reshape(R, ROWS // node_width, node_width)
        backward[height] = jnp.einsum('jba,rjb->rja', blocks, residue, precision=highest).reshape(R, ROWS)
    return jnp.stack(forward), jnp.stack(backward)
```

```python
import jax
import jax.numpy as jnp
from jax import lax
from jax.experimental import pallas as pl
from jax.experimental.pallas import tpu as pltpu
from jax.sharding import PartitionSpec as P

MESH = pl.DeviceIdType.MESH
LANES = 128
ONE_STEP = 3
NN = (((1,), (0,)), ((), ()))
NT = (((1,), (1,)), ((), ()))


def pair_slot(source, ancestor):
    return ancestor * (ancestor - 1) // 2 + source


def split(value):
    high = value.astype(jnp.bfloat16)
    low = (value - high.astype(jnp.float32)).astype(jnp.bfloat16)
    return high, low


def product(value, high, low, dims):
    rows = value.shape[0]
    value_high, value_low = split(value)
    both = lax.dot_general(
        jnp.concatenate([value_high, value_low], axis=0), high, dims, preferred_element_type=jnp.float32
    )
    rest = lax.dot_general(value_high, low, dims, preferred_element_type=jnp.float32)
    return both[:rows] + both[rows:] + rest


def scratch_plan(levels, pairs, rows, cols, group, slots):
    f32, bf16 = jnp.float32, jnp.bfloat16
    tile = (group, LANES)
    plan = {
        "diag32": pltpu.VMEM((2, rows, cols), f32),
        "off32": pltpu.VMEM((pairs, 2 * rows, 2 * LANES), f32),
        "diag_high": pltpu.VMEM((2 * rows, rows * 2**levels), bf16),
        "diag_low": pltpu.VMEM((2 * rows, rows * 2**levels), bf16),
        "off_high": pltpu.VMEM((pairs, 2 * rows, 2 * LANES), bf16),
        "off_low": pltpu.VMEM((pairs, 2 * rows, 2 * LANES), bf16),
        "tiles_v": pltpu.VMEM((2, 8, LANES), jnp.int32),
        "tiles_s": pltpu.SMEM((2, 8, LANES), jnp.int32),
    }
    for name in ("side", "fwd", "sol"):
        plan[name + "_out"] = pltpu.VMEM((slots,) + tile, f32)
        plan[name + "_in"] = pltpu.VMEM((slots,) + tile, f32)
    for name in ("b", "y", "w", "x"):
        plan[name] = pltpu.VMEM((levels,) + tile, f32)
    moves = ["side", "fwd", "sol", "diag0", "diag1", "off0", "off1", "tiles"]
    for level in range(1, levels):
        count = 2 ** (level - 1)
        plan[f"acc{level}"] = pltpu.VMEM((count,) + tile, f32)
        plan[f"full{level}"] = pltpu.VMEM((count,) + tile, f32)
        if level < 2:
            continue
        plan[f"part{level}"] = pltpu.VMEM((count,) + tile, f32)
        if level <= ONE_STEP:
            plan[f"up{level}"] = pltpu.VMEM((count, count) + tile, f32)
            plan[f"down{level}"] = pltpu.VMEM((count, count) + tile, f32)
            moves += [f"up{level}", f"down{level}"]
        else:
            plan[f"up{level}"] = pltpu.VMEM((count,) + tile, f32)
            plan[f"down{level}"] = pltpu.VMEM((count,) + tile, f32)
            plan[f"sum{level}"] = pltpu.VMEM((count,) + tile, f32)
            moves += [f"up{level}", f"down{level}", f"sum{level}", f"full{level}"]
    plan["send_sem"] = pltpu.SemaphoreType.DMA((len(moves),))
    plan["recv_sem"] = pltpu.SemaphoreType.DMA((len(moves),))
    plan["local_sem"] = pltpu.SemaphoreType.DMA((5,))
    return plan, moves


def make_kernel(levels, names, moves, rows, cols, group, grid):
    chunk = rows // grid
    slots = 2 * grid
    top = levels - 1
    chips = 2 ** (top - 1)
    low_cols = 1024
    low_pairs = 6

    def kernel(side_ref, diag_hbm, off_hbm, tile_ref, fwd_ref, sol_ref, *scratch):
        at = dict(zip(names, scratch))
        send_sem, recv_sem, local_sem = at["send_sem"], at["recv_sem"], at["local_sem"]
        slot_of = {name: place for place, name in enumerate(moves)}
        leaf, z = lax.axis_index("leaf"), lax.axis_index("grid")
        core = lax.rem(leaf, 2)
        chip = leaf // 2
        lane = lax.broadcasted_iota(jnp.int32, (group, LANES), 1)
        lane_block = lane // chunk
        left_half = lane < rows
        own_rhs = 2 * z + core
        own_rows = core * grid + z

        def column_peer(step):
            index = lax.rem(own_rhs + step, slots)
            return index, (2 * chip + lax.rem(index, 2), index // 2)

        def row_peer(step):
            index = lax.rem(own_rows + step, slots)
            return index, (2 * chip + index // grid, lax.rem(index, grid))

        def plane_peer(count, step):
            place = lax.rem(chip, count)
            index = lax.rem(place + step, count)
            return index, (2 * (chip - place + index) + core, z)

        def send(name, source, target, device):
            pltpu.make_async_remote_copy(
                src_ref=source,
                dst_ref=target,
                send_sem=send_sem.at[slot_of[name]],
                recv_sem=recv_sem.at[slot_of[name]],
                device_id=device,
                device_id_type=MESH,
            ).start()

        def await_bytes(view, sem):
            pltpu.make_async_copy(view, view, sem).wait()

        sent = []

        def received(name, view):
            await_bytes(view, recv_sem.at[slot_of[name]])
            sent.append((name, view))

        diag32, off32 = at["diag32"], at["off32"]
        low = pl.ds(0, low_cols)
        high = pl.ds(low_cols, cols - low_cols)
        mine = pl.ds(pl.multiple_of(core * rows, rows), rows)
        pairs = off_hbm.shape[0]
        low_p, high_p = pl.ds(0, low_pairs), pl.ds(low_pairs, pairs - low_pairs)
        parts = [
            ("diag0", diag_hbm.at[:, low], diag32.at[core, :, low]),
            ("off0", off_hbm.at[low_p], off32.at[low_p, mine, :]),
            ("off1", off_hbm.at[high_p], off32.at[high_p, mine, :]),
            ("diag1", diag_hbm.at[:, high], diag32.at[core, :, high]),
        ]
        own_copies = {}
        for place, (name, source, target) in enumerate(parts):
            own_copies[name] = pltpu.make_async_copy(source, target, local_sem.at[place])
            own_copies[name].start()

        barrier = pltpu.get_barrier_semaphore()

        def greet_column(step, carry):
            _, device = column_peer(step)
            pl.semaphore_signal(barrier, inc=1, device_id=device, device_id_type=MESH)
            return carry

        def greet_plane(step, carry):
            _, device = plane_peer(chips, step)
            pl.semaphore_signal(barrier, inc=1, device_id=device, device_id_type=MESH)
            return carry

        lax.fori_loop(1, slots, greet_column, 0)
        lax.fori_loop(1, chips, greet_plane, 0)

        used = levels * chunk
        side = side_ref[...].reshape(used, slots * group)
        side = jnp.concatenate([side, jnp.zeros((LANES - used, slots * group), jnp.float32)], axis=0)
        at["side_out"][...] = side.T.reshape(slots, group, LANES)
        at["tiles_v"][core] = tile_ref[...]
        for level in range(1, levels):
            at[f"acc{level}"][...] = jnp.zeros_like(at[f"acc{level}"])
        at["w"][...] = jnp.zeros_like(at["w"])

        pl.semaphore_wait(barrier, slots - 1 + chips - 1)

        def send_side(step, carry):
            index, device = column_peer(step)
            send("side", at["side_out"].at[index], at["side_in"].at[own_rows], device)
            return carry

        partner = (2 * chip + 1 - core, z)
        send("tiles", tile_ref, at["tiles_v"].at[core], partner)
        name, source, target = parts[0]
        send(name, source, target, partner)
        lax.fori_loop(1, slots, send_side, 0)
        for name, source, target in parts[1:]:
            send(name, source, target, partner)
        at["side_in"][own_rows] = at["side_out"][own_rhs]

        other = pl.ds(pl.multiple_of((1 - core) * rows, rows), rows)
        theirs = {
            "diag0": diag32.at[1 - core, :, low],
            "off0": off32.at[low_p, other, :],
            "off1": off32.at[high_p, other, :],
            "diag1": diag32.at[1 - core, :, high],
        }

        def arrived(name):
            own_copies[name].wait()
            received(name, theirs[name])

        def put_diag(half, place, value):
            value_high, value_low = split(value)
            spot = pl.ds(half * rows, rows)
            at["diag_high"][spot, place] = value_high
            at["diag_low"][spot, place] = value_low

        wide_lane = lax.broadcasted_iota(jnp.int32, (rows, LANES), 1)

        def convert_diag(first, last):
            def block(j, carry):
                here = pl.ds(pl.multiple_of(j * LANES, LANES), LANES)
                before = pl.ds(pl.multiple_of((j - 1) * LANES, LANES), LANES)
                for half in range(2):
                    mixed = jnp.where(wide_lane < rows, diag32[half, :, here], diag32[half, :, before])
                    put_diag(half, here, pltpu.roll(mixed, rows, 1))
                return carry

            lax.fori_loop(first, last, block, 0)

        def convert_last_diag():
            j = cols // LANES
            for half in range(2):
                tail = diag32[half, :, j * LANES : cols]
                tail = jnp.concatenate([tail, jnp.zeros((rows, LANES - rows), jnp.float32)], axis=1)
                mixed = jnp.where(wide_lane < rows, tail, diag32[half, :, (j - 1) * LANES : j * LANES])
                put_diag(half, pl.ds(j * LANES, LANES), pltpu.roll(mixed, rows, 1))

        def convert_off(first, last):
            def block(p, carry):
                value_high, value_low = split(off32[p])
                at["off_high"][p] = value_high
                at["off_low"][p] = value_low
                return carry

            lax.fori_loop(first, last, block, 0)

        arrived("diag0")
        for half in range(2):
            first = jnp.where(wide_lane < rows, diag32[half, :, 0:LANES], 0.0)
            put_diag(half, pl.ds(0, LANES), first if half == 0 else pltpu.roll(first, rows, 1))
        convert_diag(1, low_cols // LANES)
        arrived("off0")
        convert_off(0, low_pairs)
        received("tiles", at["tiles_v"].at[1 - core])
        to_smem = pltpu.make_async_copy(at["tiles_v"], at["tiles_s"], local_sem.at[4])
        to_smem.start()
        to_smem.wait()
        tiles = at["tiles_s"]

        received("side", at["side_in"].at[pl.ds(0, slots - 1)])
        turned = []
        for s in range(slots):
            value = at["side_in"][s]
            turned.append(pltpu.roll(value, s * chunk, 1) if s else value)
        for level in range(levels):
            value = turned[0]
            for s in range(1, slots):
                value = jnp.where(lane_block == (s + level) % slots, turned[s], value)
            at["b"][level] = pltpu.roll(value, LANES - level * chunk, 1) if level else value

        def diag_block(level):
            if level == 0:
                place = pl.ds(0, LANES)
            else:
                place = pl.ds(rows * 2**level, rows * 2**level)
            return at["diag_high"][:, place], at["diag_low"][:, place]

        def contribute(source, level):
            p = pair_slot(source, level)
            known = at["y"][source]
            stacked = jnp.concatenate([jnp.where(left_half, known, 0.0), jnp.where(left_half, 0.0, known)], axis=0)
            out = product(stacked, at["off_high"][p], at["off_low"][p], NN)
            pieces = []
            for half in range(2):
                for t in range(2):
                    piece = out[half * group : (half + 1) * group, t * LANES : (t + 1) * LANES]
                    pieces.append((piece, tiles[half, t, p]))
            acc = at[f"acc{level}"]
            count = 2 ** (level - 1)

            def add(target, carry):
                value = acc[target]
                for piece, number in pieces:
                    value = value - piece * (number == target).astype(jnp.float32)
                acc[target] = value
                return carry

            if count <= 4:
                for target in range(count):
                    add(target, 0)
            else:
                lax.fori_loop(0, count, add, 0)

        def gather_known(ancestor, level):
            p = pair_slot(level, ancestor)
            full = at[f"full{ancestor}"]
            halves = []
            for half in range(2):
                halves.append(jnp.concatenate([full[tiles[half, t, p]] for t in range(2)], axis=1))
            out = product(jnp.concatenate(halves, axis=0), at["off_high"][p], at["off_low"][p], NT)
            at["w"][level] += jnp.where(left_half, out[:group], out[group:])

        def broadcast(name, source, level):
            count = 2 ** (level - 1)
            place = lax.rem(chip, count)
            target = at[name]

            def one(step, carry):
                _, device = plane_peer(count, step)
                send(name, source, target.at[place], device)
                return carry

            lax.fori_loop(1, count, one, 0)

        def scatter(name, source, level):
            count = 2 ** (level - 1)
            place = lax.rem(chip, count)
            target = at[name]

            def one(step, carry):
                index, device = plane_peer(count, step)
                send(name, source.at[index], target.at[place], device)
                return carry

            lax.fori_loop(1, count, one, 0)

        def await_all(name, level):
            count = 2 ** (level - 1)
            received(name, at[name].at[pl.ds(0, count - 1)])

        def total(ref, count):
            value = ref[0]
            for place in range(1, count):
                value = value + ref[place]
            return value

        at["y"][0] = product(at["b"][0], *diag_block(0), NT)
        contribute(0, 1)
        at["y"][1] = product(at["b"][1] + at["acc1"][0], *diag_block(1), NT)
        contribute(0, 2)
        for level in range(2, levels):
            count = 2 ** (level - 1)
            place = lax.rem(chip, count)
            contribute(level - 1, level)
            acc, up = at[f"acc{level}"], at[f"up{level}"]
            if level <= ONE_STEP:
                acc[place] += at["b"][level]
                broadcast(f"up{level}", acc, level)
                up[place] = acc[...]
            else:
                scatter(f"up{level}", acc, level)
                up[place] = acc[place]
            if level == 2:
                for source in range(level):
                    contribute(source, level + 1) if level < top else None
                arrived("off1")
                convert_off(low_pairs, pairs)
            else:
                if level < top:
                    for source in range(level):
                        contribute(source, level + 1)
                if level == 3:
                    arrived("diag1")
                    convert_diag(low_cols // LANES, 2 * low_cols // LANES)
            await_all(f"up{level}", level)
            if level <= ONE_STEP:
                whole = total(up, count)
            else:
                summed = at[f"sum{level}"]
                summed[place] = at["b"][level] + total(up, count)
                broadcast(f"sum{level}", summed.at[place], level)
                if level == top - 2:
                    convert_diag(rows * 2 ** (level + 1) // LANES, rows * 2 ** (level + 2) // LANES)
                if level == top - 1:
                    convert_diag(rows * 2 ** (level + 1) // LANES, rows * 2 ** (level + 2) // LANES - 1)
                    convert_last_diag()
                await_all(f"sum{level}", level)
                whole = summed[...]
            whole = jnp.concatenate([whole[t] for t in range(count)], axis=1)
            at["y"][level] = product(whole, *diag_block(level), NT)

        def pack(values, name):
            turned = []
            for level in range(levels):
                value = values[level]
                turned.append(pltpu.roll(value, level * chunk, 1) if level else value)
            for s in range(slots):
                value = turned[0]
                for level in range(1, levels):
                    value = jnp.where(lane_block == (s + level) % slots, turned[level], value)
                at[name + "_out"][s] = pltpu.roll(value, LANES - s * chunk, 1) if s else value

            def one(step, carry):
                index, device = row_peer(step)
                send(name, at[name + "_out"].at[index], at[name + "_in"].at[own_rhs], device)
                return carry

            lax.fori_loop(1, slots, one, 0)
            at[name + "_in"][own_rhs] = at[name + "_out"][own_rows]

        def unpack(name, target):
            received(name, at[name + "_in"].at[pl.ds(0, slots - 1)])
            value = at[name + "_in"][...].reshape(slots * group, LANES).T
            for level in range(levels):
                target[level] = value[level * chunk : (level + 1) * chunk]

        for level in reversed(range(levels)):
            residue = at["y"][level] - at["w"][level]
            value = product(residue, *diag_block(level), NN)
            if level < 2:
                at["x"][level] = value
                if level == 1:
                    at["full1"][0] = value
                    gather_known(1, 0)
                continue
            count = 2 ** (level - 1)
            place = lax.rem(chip, count)
            part, down, full = at[f"part{level}"], at[f"down{level}"], at[f"full{level}"]
            for t in range(count):
                part[t] = value[:, t * LANES : (t + 1) * LANES]
            later = [(level + 1, below) for below in reversed(range(level))] if level < top else []
            if level <= ONE_STEP:
                broadcast(f"down{level}", part, level)
                down[place] = part[...]
                for task in later:
                    gather_known(*task)
                await_all(f"down{level}", level)
                full[...] = total(down, count)
                at["x"][level] = full[place]
            else:
                scatter(f"down{level}", part, level)
                down[place] = part[place]
                if level == top:
                    pack(at["y"], "fwd")
                for task in later[:1]:
                    gather_known(*task)
                await_all(f"down{level}", level)
                value = total(down, count)
                at["x"][level] = value
                full[place] = value
                broadcast(f"full{level}", full.at[place], level)
                for task in later[1:]:
                    gather_known(*task)
                if level == top:
                    unpack("fwd", fwd_ref)
                await_all(f"full{level}", level)
            gather_known(level, level - 1)
            if level == 2:
                gather_known(2, 0)
        pack(at["x"], "sol")
        unpack("sol", sol_ref)
        for name, view in sent:
            await_bytes(view, send_sem.at[slot_of[name]])

    return kernel


def solution(mesh):
    grid = mesh.shape["grid"]

    def local(right_side, diag_inv, off_diag, tile_rows):
        levels, rhs, chunk = right_side.shape
        rows, cols = diag_inv.shape
        pairs = off_diag.shape[0]
        slots = 2 * grid
        group = rhs // slots
        side = jnp.transpose(right_side, (0, 2, 1))
        off = jnp.transpose(off_diag, (0, 2, 1))
        tiles = jnp.transpose(tile_rows[:, :, 0], (1, 0))
        tiles = jnp.pad(tiles, ((0, 8 - tiles.shape[0]), (0, LANES - pairs)))
        plan, moves = scratch_plan(levels, pairs, rows, cols, group, slots)
        vmem = pl.BlockSpec(memory_space=pltpu.VMEM)
        anywhere = pl.BlockSpec(memory_space=pl.ANY)
        out = jax.ShapeDtypeStruct(side.shape, jnp.float32)
        forward, backward = pl.pallas_call(
            make_kernel(levels, list(plan), moves, rows, cols, group, grid),
            out_shape=(out, out),
            in_specs=[vmem, anywhere, anywhere, vmem],
            out_specs=(vmem, vmem),
            scratch_shapes=list(plan.values()),
            compiler_params=pltpu.CompilerParams(
                collective_id=0, has_side_effects=True, vmem_limit_bytes=48 * 2**20
            ),
            name="tree_solve",
        )(side, diag_inv, off, tiles)
        return jnp.transpose(forward, (0, 2, 1)), jnp.transpose(backward, (0, 2, 1))

    in_specs = (
        P(None, None, ("leaf", "grid")),
        P("leaf", None),
        P(None, None, "leaf"),
        P(None, None, "leaf"),
    )
    out_specs = (P(None, None, ("leaf", "grid")), P(None, None, ("leaf", "grid")))
    return jax.shard_map(local, mesh=mesh, in_specs=in_specs, out_specs=out_specs, check_vma=False)
```

```python
import jax
import jax.numpy as jnp
from jax import lax
from jax.experimental import pallas as pl
from jax.experimental.pallas import tpu as pltpu
from jax.sharding import PartitionSpec as P

MESH = pl.DeviceIdType.MESH
LANES = 128
ONE_STEP = 3
NN = (((1,), (0,)), ((), ()))
NT = (((1,), (1,)), ((), ()))


def pair_slot(source, ancestor):
    return ancestor * (ancestor - 1) // 2 + source


def outward(place, size):
    away = (place + 1) // 2
    return lax.rem(size // 2 + away * (1 - 2 * lax.rem(place, 2)) + size, size)


def split(value):
    high = value.astype(jnp.bfloat16)
    low = (value - high.astype(jnp.float32)).astype(jnp.bfloat16)
    return high, low


def product(value, high, low, dims):
    rows = value.shape[0]
    value_high, value_low = split(value)
    both = lax.dot_general(
        jnp.concatenate([value_high, value_low], axis=0), high, dims, preferred_element_type=jnp.float32
    )
    rest = lax.dot_general(value_high, low, dims, preferred_element_type=jnp.float32)
    return both[:rows] + both[rows:] + rest


def scratch_plan(levels, pairs, rows, cols, group, slots):
    f32, bf16 = jnp.float32, jnp.bfloat16
    tile = (group, LANES)
    plan = {
        "diag32": pltpu.VMEM((2, rows, cols), f32),
        "off32": pltpu.VMEM((pairs, 2 * rows, 2 * LANES), f32),
        "diag_high": pltpu.VMEM((2 * rows, rows * 2**levels), bf16),
        "diag_low": pltpu.VMEM((2 * rows, rows * 2**levels), bf16),
        "off_high": pltpu.VMEM((pairs, 2 * rows, 2 * LANES), bf16),
        "off_low": pltpu.VMEM((pairs, 2 * rows, 2 * LANES), bf16),
        "tiles_v": pltpu.VMEM((2, 2, pairs), jnp.int32),
        "tiles_s": pltpu.SMEM((2, 2, pairs), jnp.int32),
    }
    plan["side32"] = pltpu.VMEM((levels, rows // (slots // 2), slots * group), f32)
    for name in ("side", "fwd", "sol"):
        plan[name + "_out"] = pltpu.VMEM((slots,) + tile, f32)
        plan[name + "_in"] = pltpu.VMEM((slots,) + tile, f32)
    for name in ("b", "y", "w", "x"):
        plan[name] = pltpu.VMEM((levels,) + tile, f32)
    moves = ["side", "fwd", "sol", "diag0", "diag1", "off0", "off1", "tiles"]
    for level in range(1, levels):
        count = 2 ** (level - 1)
        plan[f"acc{level}"] = pltpu.VMEM((count,) + tile, f32)
        plan[f"full{level}"] = pltpu.VMEM((count,) + tile, f32)
        if level < 2:
            continue
        plan[f"part{level}"] = pltpu.VMEM((count,) + tile, f32)
        if level <= ONE_STEP:
            plan[f"up{level}"] = pltpu.VMEM((count, count) + tile, f32)
            plan[f"down{level}"] = pltpu.VMEM((count, count) + tile, f32)
            moves += [f"up{level}", f"down{level}"]
        else:
            plan[f"up{level}"] = pltpu.VMEM((count,) + tile, f32)
            plan[f"down{level}"] = pltpu.VMEM((count,) + tile, f32)
            plan[f"sum{level}"] = pltpu.VMEM((count,) + tile, f32)
            moves += [f"up{level}", f"down{level}", f"sum{level}", f"full{level}"]
    plan["send_sem"] = pltpu.SemaphoreType.DMA((len(moves),))
    plan["recv_sem"] = pltpu.SemaphoreType.DMA((len(moves),))
    plan["local_sem"] = pltpu.SemaphoreType.DMA((7,))
    return plan, moves


def make_kernel(levels, names, moves, rows, cols, group, grid):
    chunk = rows // grid
    slots = 2 * grid
    top = levels - 1
    chips = 2 ** (top - 1)
    low_cols = 1024
    low_pairs = 6
    ring = min(8, chips)

    def kernel(side_hbm, diag_hbm, off_hbm, tile_hbm, fwd_ref, sol_ref, *scratch):
        at = dict(zip(names, scratch))
        send_sem, recv_sem, local_sem = at["send_sem"], at["recv_sem"], at["local_sem"]
        slot_of = {name: place for place, name in enumerate(moves)}
        leaf, z = lax.axis_index("leaf"), lax.axis_index("grid")
        core = lax.rem(leaf, 2)
        chip = leaf // 2
        lane = lax.broadcasted_iota(jnp.int32, (group, LANES), 1)
        lane_block = lane // chunk
        left_half = lane < rows
        own_rhs = 2 * z + core
        own_rows = core * grid + z

        def column_device(step):
            their_z = lax.rem(z + outward(step // 2, grid), grid)
            their_core = lax.rem(core + 1 + lax.rem(step, 2), 2)
            return their_core, their_z, (2 * chip + their_core, their_z)

        def column_peer(step):
            their_core, their_z, device = column_device(step)
            return 2 * their_z + their_core, device

        def row_peer(step):
            their_core, their_z, device = column_device(step)
            return their_core * grid + their_z, device

        def plane_peer(count, step):
            place = lax.rem(chip, count)
            if count < ring:
                index = lax.rem(place + outward(step, count), count)
            else:
                lines = count // ring
                line = lax.rem(place // ring + outward(lax.rem(step, lines), lines), lines)
                index = line * ring + lax.rem(place + outward(step // lines, ring), ring)
            return index, (2 * (chip - place + index) + core, z)

        def send(name, source, target, device):
            pltpu.make_async_remote_copy(
                src_ref=source,
                dst_ref=target,
                send_sem=send_sem.at[slot_of[name]],
                recv_sem=recv_sem.at[slot_of[name]],
                device_id=device,
                device_id_type=MESH,
            ).start()

        def await_bytes(view, sem):
            pltpu.make_async_copy(view, view, sem).wait()

        sent = []

        def received(name, view):
            await_bytes(view, recv_sem.at[slot_of[name]])
            sent.append((name, view))

        diag32, off32 = at["diag32"], at["off32"]
        low = pl.ds(0, low_cols)
        high = pl.ds(low_cols, cols - low_cols)
        mine = pl.ds(pl.multiple_of(core * rows, rows), rows)
        pairs = off_hbm.shape[0]
        low_p, high_p = pl.ds(0, low_pairs), pl.ds(low_pairs, pairs - low_pairs)
        load_side = pltpu.make_async_copy(side_hbm, at["side32"], local_sem.at[5])
        load_side.start()
        load_tiles = pltpu.make_async_copy(tile_hbm, at["tiles_v"].at[core], local_sem.at[6])
        load_tiles.start()
        parts = [
            ("diag0", diag_hbm.at[:, low], diag32.at[core, :, low]),
            ("off0", off_hbm.at[low_p], off32.at[low_p, mine, :]),
            ("off1", off_hbm.at[high_p], off32.at[high_p, mine, :]),
            ("diag1", diag_hbm.at[:, high], diag32.at[core, :, high]),
        ]
        own_copies = {}
        for place, (name, source, target) in enumerate(parts):
            own_copies[name] = pltpu.make_async_copy(source, target, local_sem.at[place])
            own_copies[name].start()

        barrier = pltpu.get_barrier_semaphore()

        def greet_column(step, carry):
            _, device = column_peer(step)
            pl.semaphore_signal(barrier, inc=1, device_id=device, device_id_type=MESH)
            return carry

        def greet_plane(step, carry):
            _, device = plane_peer(chips, step)
            pl.semaphore_signal(barrier, inc=1, device_id=device, device_id_type=MESH)
            return carry

        lax.fori_loop(0, slots - 1, greet_column, 0)
        lax.fori_loop(0, chips - 1, greet_plane, 0)

        used = levels * chunk
        load_side.wait()
        side = at["side32"][...].reshape(used, slots * group)
        side = jnp.concatenate([side, jnp.zeros((LANES - used, slots * group), jnp.float32)], axis=0)
        at["side_out"][...] = side.T.reshape(slots, group, LANES)
        for level in range(1, levels):
            at[f"acc{level}"][...] = jnp.zeros_like(at[f"acc{level}"])
        at["w"][...] = jnp.zeros_like(at["w"])

        pl.semaphore_wait(barrier, slots - 1 + chips - 1)

        def send_side(step, carry):
            index, device = column_peer(step)
            send("side", at["side_out"].at[index], at["side_in"].at[own_rows], device)
            return carry

        partner = (2 * chip + 1 - core, z)
        send("tiles", tile_hbm, at["tiles_v"].at[core], partner)
        lax.fori_loop(0, slots - 1, send_side, 0)
        for name, source, target in parts:
            send(name, source, target, partner)
        at["side_in"][own_rows] = at["side_out"][own_rhs]

        other = pl.ds(pl.multiple_of((1 - core) * rows, rows), rows)
        theirs = {
            "diag0": diag32.at[1 - core, :, low],
            "off0": off32.at[low_p, other, :],
            "off1": off32.at[high_p, other, :],
            "diag1": diag32.at[1 - core, :, high],
        }

        def arrived(name):
            own_copies[name].wait()
            received(name, theirs[name])

        def put_diag(half, place, value):
            value_high, value_low = split(value)
            spot = pl.ds(half * rows, rows)
            at["diag_high"][spot, place] = value_high
            at["diag_low"][spot, place] = value_low

        wide_lane = lax.broadcasted_iota(jnp.int32, (rows, LANES), 1)

        def convert_diag(first, last):
            def block(j, carry):
                here = pl.ds(pl.multiple_of(j * LANES, LANES), LANES)
                before = pl.ds(pl.multiple_of((j - 1) * LANES, LANES), LANES)
                for half in range(2):
                    mixed = jnp.where(wide_lane < rows, diag32[half, :, here], diag32[half, :, before])
                    put_diag(half, here, pltpu.roll(mixed, rows, 1))
                return carry

            lax.fori_loop(first, last, block, 0)

        def convert_last_diag():
            j = cols // LANES
            for half in range(2):
                tail = diag32[half, :, j * LANES : cols]
                tail = jnp.concatenate([tail, jnp.zeros((rows, LANES - rows), jnp.float32)], axis=1)
                mixed = jnp.where(wide_lane < rows, tail, diag32[half, :, (j - 1) * LANES : j * LANES])
                put_diag(half, pl.ds(j * LANES, LANES), pltpu.roll(mixed, rows, 1))

        def convert_off(first, last):
            def block(p, carry):
                value_high, value_low = split(off32[p])
                at["off_high"][p] = value_high
                at["off_low"][p] = value_low
                return carry

            lax.fori_loop(first, last, block, 0)

        arrived("diag0")
        for half in range(2):
            first = jnp.where(wide_lane < rows, diag32[half, :, 0:LANES], 0.0)
            put_diag(half, pl.ds(0, LANES), first if half == 0 else pltpu.roll(first, rows, 1))
        convert_diag(1, low_cols // LANES)
        arrived("off0")
        convert_off(0, low_pairs)
        load_tiles.wait()
        received("tiles", at["tiles_v"].at[1 - core])
        to_smem = pltpu.make_async_copy(at["tiles_v"], at["tiles_s"], local_sem.at[4])
        to_smem.start()
        to_smem.wait()
        tiles = at["tiles_s"]

        received("side", at["side_in"].at[pl.ds(0, slots - 1)])
        turned = []
        for s in range(slots):
            value = at["side_in"][s]
            turned.append(pltpu.roll(value, s * chunk, 1) if s else value)
        for level in range(levels):
            value = turned[0]
            for s in range(1, slots):
                value = jnp.where(lane_block == (s + level) % slots, turned[s], value)
            at["b"][level] = pltpu.roll(value, LANES - level * chunk, 1) if level else value

        def diag_block(level):
            if level == 0:
                place = pl.ds(0, LANES)
            else:
                place = pl.ds(rows * 2**level, rows * 2**level)
            return at["diag_high"][:, place], at["diag_low"][:, place]

        def contribute(source, level):
            p = pair_slot(source, level)
            known = at["y"][source]
            stacked = jnp.concatenate([jnp.where(left_half, known, 0.0), jnp.where(left_half, 0.0, known)], axis=0)
            out = product(stacked, at["off_high"][p], at["off_low"][p], NN)
            pieces = []
            for half in range(2):
                for t in range(2):
                    piece = out[half * group : (half + 1) * group, t * LANES : (t + 1) * LANES]
                    pieces.append((piece, tiles[half, t, p]))
            acc = at[f"acc{level}"]
            count = 2 ** (level - 1)

            def add(target, carry):
                value = acc[target]
                for piece, number in pieces:
                    value = value - piece * (number == target).astype(jnp.float32)
                acc[target] = value
                return carry

            if count <= 4:
                for target in range(count):
                    add(target, 0)
            else:
                lax.fori_loop(0, count, add, 0)

        def gather_known(ancestor, level):
            p = pair_slot(level, ancestor)
            full = at[f"full{ancestor}"]
            halves = []
            for half in range(2):
                halves.append(jnp.concatenate([full[tiles[half, t, p]] for t in range(2)], axis=1))
            out = product(jnp.concatenate(halves, axis=0), at["off_high"][p], at["off_low"][p], NT)
            at["w"][level] += jnp.where(left_half, out[:group], out[group:])

        def broadcast(name, source, level):
            count = 2 ** (level - 1)
            place = lax.rem(chip, count)
            target = at[name]

            def one(step, carry):
                _, device = plane_peer(count, step)
                send(name, source, target.at[place], device)
                return carry

            lax.fori_loop(0, count - 1, one, 0)

        def scatter(name, source, level):
            count = 2 ** (level - 1)
            place = lax.rem(chip, count)
            target = at[name]

            def one(step, carry):
                index, device = plane_peer(count, step)
                send(name, source.at[index], target.at[place], device)
                return carry

            lax.fori_loop(0, count - 1, one, 0)

        def await_all(name, level):
            count = 2 ** (level - 1)
            received(name, at[name].at[pl.ds(0, count - 1)])

        def total(ref, count):
            value = ref[0]
            for place in range(1, count):
                value = value + ref[place]
            return value

        at["y"][0] = product(at["b"][0], *diag_block(0), NT)
        contribute(0, 1)
        at["y"][1] = product(at["b"][1] + at["acc1"][0], *diag_block(1), NT)
        contribute(0, 2)
        for level in range(2, levels):
            count = 2 ** (level - 1)
            place = lax.rem(chip, count)
            contribute(level - 1, level)
            acc, up = at[f"acc{level}"], at[f"up{level}"]
            if level <= ONE_STEP:
                acc[place] += at["b"][level]
                broadcast(f"up{level}", acc, level)
                up[place] = acc[...]
            else:
                scatter(f"up{level}", acc, level)
                up[place] = acc[place]
            if level == 2:
                for source in range(level):
                    contribute(source, level + 1) if level < top else None
                arrived("off1")
                convert_off(low_pairs, pairs)
            else:
                if level < top:
                    for source in range(level):
                        contribute(source, level + 1)
                if level == 3:
                    arrived("diag1")
                    convert_diag(low_cols // LANES, 2 * low_cols // LANES)
            await_all(f"up{level}", level)
            if level <= ONE_STEP:
                whole = total(up, count)
            else:
                summed = at[f"sum{level}"]
                summed[place] = at["b"][level] + total(up, count)
                broadcast(f"sum{level}", summed.at[place], level)
                if level == top - 2:
                    convert_diag(rows * 2 ** (level + 1) // LANES, rows * 2 ** (level + 2) // LANES)
                if level == top - 1:
                    convert_diag(rows * 2 ** (level + 1) // LANES, rows * 2 ** (level + 2) // LANES - 1)
                    convert_last_diag()
                await_all(f"sum{level}", level)
                whole = summed[...]
            whole = jnp.concatenate([whole[t] for t in range(count)], axis=1)
            at["y"][level] = product(whole, *diag_block(level), NT)

        def pack(values, name):
            turned = []
            for level in range(levels):
                value = values[level]
                turned.append(pltpu.roll(value, level * chunk, 1) if level else value)
            for s in range(slots):
                value = turned[0]
                for level in range(1, levels):
                    value = jnp.where(lane_block == (s + level) % slots, turned[level], value)
                at[name + "_out"][s] = pltpu.roll(value, LANES - s * chunk, 1) if s else value

            def one(step, carry):
                index, device = row_peer(step)
                send(name, at[name + "_out"].at[index], at[name + "_in"].at[own_rhs], device)
                return carry

            lax.fori_loop(0, slots - 1, one, 0)
            at[name + "_in"][own_rhs] = at[name + "_out"][own_rows]

        def unpack(name, target):
            received(name, at[name + "_in"].at[pl.ds(0, slots - 1)])
            value = at[name + "_in"][...].reshape(slots * group, LANES).T
            for level in range(levels):
                target[level] = value[level * chunk : (level + 1) * chunk]

        for level in reversed(range(levels)):
            residue = at["y"][level] - at["w"][level]
            value = product(residue, *diag_block(level), NN)
            if level < 2:
                at["x"][level] = value
                if level == 1:
                    at["full1"][0] = value
                    gather_known(1, 0)
                continue
            count = 2 ** (level - 1)
            place = lax.rem(chip, count)
            part, down, full = at[f"part{level}"], at[f"down{level}"], at[f"full{level}"]
            for t in range(count):
                part[t] = value[:, t * LANES : (t + 1) * LANES]
            later = [(level + 1, below) for below in reversed(range(level))] if level < top else []
            if level <= ONE_STEP:
                broadcast(f"down{level}", part, level)
                down[place] = part[...]
                for task in later:
                    gather_known(*task)
                await_all(f"down{level}", level)
                full[...] = total(down, count)
                at["x"][level] = full[place]
            else:
                scatter(f"down{level}", part, level)
                down[place] = part[place]
                if level == top:
                    pack(at["y"], "fwd")
                for task in later[:1]:
                    gather_known(*task)
                await_all(f"down{level}", level)
                value = total(down, count)
                at["x"][level] = value
                full[place] = value
                broadcast(f"full{level}", full.at[place], level)
                for task in later[1:]:
                    gather_known(*task)
                if level == top:
                    unpack("fwd", fwd_ref)
                await_all(f"full{level}", level)
            gather_known(level, level - 1)
            if level == 2:
                gather_known(2, 0)
        pack(at["x"], "sol")
        unpack("sol", sol_ref)
        for name, view in sent:
            await_bytes(view, send_sem.at[slot_of[name]])

    return kernel


def solution(mesh):
    grid = mesh.shape["grid"]

    def local(right_side, diag_inv, off_diag, tile_rows):
        levels, rhs, chunk = right_side.shape
        rows, cols = diag_inv.shape
        pairs = off_diag.shape[0]
        slots = 2 * grid
        group = rhs // slots
        side = jnp.transpose(right_side, (0, 2, 1))
        off = jnp.transpose(off_diag, (0, 2, 1))
        tiles = jnp.transpose(tile_rows[:, :, 0], (1, 0))
        plan, moves = scratch_plan(levels, pairs, rows, cols, group, slots)
        vmem = pl.BlockSpec(memory_space=pltpu.VMEM)
        hbm = pl.BlockSpec(memory_space=pltpu.HBM)
        out = jax.ShapeDtypeStruct(side.shape, jnp.float32)
        forward, backward = pl.pallas_call(
            make_kernel(levels, list(plan), moves, rows, cols, group, grid),
            out_shape=(out, out),
            in_specs=[hbm, hbm, hbm, hbm],
            out_specs=(vmem, vmem),
            scratch_shapes=list(plan.values()),
            compiler_params=pltpu.CompilerParams(
                collective_id=0, has_side_effects=True, vmem_limit_bytes=48 * 2**20
            ),
            name="tree_solve",
        )(*(pltpu.with_memory_space_constraint(part, pltpu.HBM) for part in (side, diag_inv, off, tiles)))
        return jnp.transpose(forward, (0, 2, 1)), jnp.transpose(backward, (0, 2, 1))

    in_specs = (
        P(None, None, ("leaf", "grid")),
        P("leaf", None),
        P(None, None, "leaf"),
        P(None, None, "leaf"),
    )
    out_specs = (P(None, None, ("leaf", "grid")), P(None, None, ("leaf", "grid")))
    return jax.shard_map(local, mesh=mesh, in_specs=in_specs, out_specs=out_specs, check_vma=False)
```

```python
import types

import jax
import jax.numpy as jnp
from jax import lax
from jax.experimental import pallas as pl
from jax.experimental.pallas import tpu as pltpu
from jax.sharding import PartitionSpec as P

MESH = pl.DeviceIdType.MESH
LANES = 128
ONE_STEP = 3
MIX_TOP = 5
NN = (((1,), (0,)), ((), ()))
NT = (((1,), (1,)), ((), ()))


def pair_slot(source, ancestor):
    return ancestor * (ancestor - 1) // 2 + source


def outward(place, size):
    away = (place + 1) // 2
    return lax.rem(size // 2 + away * (1 - 2 * lax.rem(place, 2)) + size, size)


def split(value):
    high = value.astype(jnp.bfloat16)
    low = (value - high.astype(jnp.float32)).astype(jnp.bfloat16)
    return high, low


def product(value, high, low, dims):
    rows = value.shape[0]
    value_high, value_low = split(value)
    both = lax.dot_general(
        jnp.concatenate([value_high, value_low], axis=0), high, dims, preferred_element_type=jnp.float32
    )
    rest = lax.dot_general(value_high, low, dims, preferred_element_type=jnp.float32)
    return both[:rows] + both[rows:] + rest


def scratch_plan(levels, pairs, rows, cols, group, slots):
    f32, bf16 = jnp.float32, jnp.bfloat16
    tile = (group, LANES)
    plan = {
        ("diag32", 0): pltpu.VMEM((2, rows, cols), f32),
        ("off32", 0): pltpu.VMEM((pairs, 2 * rows, 2 * LANES), f32),
        ("diag_high", 0): pltpu.VMEM((2 * rows, rows * 2**levels), bf16),
        ("diag_low", 0): pltpu.VMEM((2 * rows, rows * 2**levels), bf16),
        ("off_high", 0): pltpu.VMEM((pairs, 2 * rows, 2 * LANES), bf16),
        ("off_low", 0): pltpu.VMEM((pairs, 2 * rows, 2 * LANES), bf16),
        ("tiles_v", 0): pltpu.VMEM((2, 2, pairs), jnp.int32),
        ("tiles_s", 0): pltpu.SMEM((2, 2, pairs), jnp.int32),
    }
    plan["side32", 0] = pltpu.VMEM((levels, rows // (slots // 2), slots * group), f32)
    for name in ("side", "fwd", "sol"):
        plan[name + "_out", 0] = pltpu.VMEM((slots,) + tile, f32)
        plan[name + "_in", 0] = pltpu.VMEM((slots,) + tile, f32)
    for name in ("b", "y", "w", "x"):
        plan[name, 0] = pltpu.VMEM((levels,) + tile, f32)
    moves = ["side", "fwd", "sol", "diag0", "diag1", "off0", "off1", "tiles", "ptiles"]
    plan["ptiles_v", 0] = pltpu.VMEM((2 ** (MIX_TOP - 1), 2, pairs), jnp.int32)
    plan["ptiles_s", 0] = pltpu.SMEM((2 ** (MIX_TOP - 1), 2, pairs), jnp.int32)
    for level in range(1, levels):
        count = 2 ** (level - 1)
        plan["acc", level] = pltpu.VMEM((count,) + tile, f32)
        plan["full", level] = pltpu.VMEM((count,) + tile, f32)
        if level < 2:
            continue
        plan["part", level] = pltpu.VMEM((count,) + tile, f32)
        if level <= ONE_STEP:
            plan["up", level] = pltpu.VMEM((count, count) + tile, f32)
            plan["down", level] = pltpu.VMEM((count, count) + tile, f32)
            moves += [("up", level), ("down", level)]
        else:
            plan["up", level] = pltpu.VMEM((count,) + tile, f32)
            plan["down", level] = pltpu.VMEM((count,) + tile, f32)
            plan["sum", level] = pltpu.VMEM((count,) + tile, f32)
            moves += [("up", level), ("down", level), ("sum", level), ("full", level)]
            if level > MIX_TOP:
                continue
            plan["mid", level] = pltpu.VMEM((count,) + tile, f32)
            plan["mpart", level] = pltpu.VMEM((count,) + tile, f32)
            plan["lrow", level] = pltpu.VMEM((count, 2 * rows // slots, 2 * LANES), f32)
            plan["mix", level] = pltpu.VMEM((count, slots, 2 * rows // slots, LANES), f32)
            plan["block_high", level] = pltpu.VMEM((count, LANES, LANES), bf16)
            plan["block_low", level] = pltpu.VMEM((count, LANES, LANES), bf16)
            plan["mix_high", level] = pltpu.VMEM((count * LANES, LANES), bf16)
            plan["mix_low", level] = pltpu.VMEM((count * LANES, LANES), bf16)
            moves += [("mid", level), ("lrow", level), ("mix", level), ("swap", level)]
            if level == MIX_TOP:
                plan["new", level] = pltpu.VMEM((count,) + tile, f32)
                moves.append(("new", level))
    plan["send_sem", 0] = pltpu.SemaphoreType.DMA((len(moves),))
    plan["recv_sem", 0] = pltpu.SemaphoreType.DMA((len(moves),))
    plan["local_sem", 0] = pltpu.SemaphoreType.DMA((8,))
    return plan, moves


def make_kernel(levels, names, moves, rows, cols, group, grid):
    chunk = rows // grid
    slots = 2 * grid
    top = levels - 1
    chips = 2 ** (top - 1)
    low_cols = 1024
    low_pairs = 6
    ring = min(8, chips)

    def kernel(side_hbm, diag_hbm, off_hbm, tile_hbm, fwd_ref, sol_ref, *scratch):
        table = dict(zip(names, scratch))
        at = types.SimpleNamespace()
        for (name, level), ref in table.items():
            if level:
                vars(at).setdefault(name, {})[level] = ref
            else:
                vars(at)[name] = ref
        send_sem, recv_sem, local_sem = at.send_sem, at.recv_sem, at.local_sem
        slot_of = {name: place for place, name in enumerate(moves)}
        leaf, z = lax.axis_index("leaf"), lax.axis_index("grid")
        core = lax.rem(leaf, 2)
        chip = leaf // 2
        lane = lax.broadcasted_iota(jnp.int32, (group, LANES), 1)
        lane_block = lane // chunk
        left_half = lane < rows
        own_rhs = 2 * z + core
        own_rows = core * grid + z

        def column_device(step):
            their_z = lax.rem(z + outward(step // 2, grid), grid)
            their_core = lax.rem(core + 1 + lax.rem(step, 2), 2)
            return their_core, their_z, (2 * chip + their_core, their_z)

        def column_peer(step):
            their_core, their_z, device = column_device(step)
            return 2 * their_z + their_core, device

        def row_peer(step):
            their_core, their_z, device = column_device(step)
            return their_core * grid + their_z, device

        def plane_peer(count, step):
            place = lax.rem(chip, count)
            if count < ring:
                index = lax.rem(place + outward(step, count), count)
            else:
                lines = count // ring
                line = lax.rem(place // ring + outward(lax.rem(step, lines), lines), lines)
                index = line * ring + lax.rem(place + outward(step // lines, ring), ring)
            return index, (2 * (chip - place + index) + core, z)

        def send(name, source, target, device):
            pltpu.make_async_remote_copy(
                src_ref=source,
                dst_ref=target,
                send_sem=send_sem.at[slot_of[name]],
                recv_sem=recv_sem.at[slot_of[name]],
                device_id=device,
                device_id_type=MESH,
            ).start()

        def await_bytes(view, sem):
            pltpu.make_async_copy(view, view, sem).wait()

        sent = []

        def received(name, view):
            await_bytes(view, recv_sem.at[slot_of[name]])
            sent.append((name, view))

        diag32, off32 = at.diag32, at.off32
        low = pl.ds(0, low_cols)
        high = pl.ds(low_cols, cols - low_cols)
        mine = pl.ds(pl.multiple_of(core * rows, rows), rows)
        pairs = off_hbm.shape[0]
        low_p, high_p = pl.ds(0, low_pairs), pl.ds(low_pairs, pairs - low_pairs)
        load_side = pltpu.make_async_copy(side_hbm, at.side32, local_sem.at[5])
        load_side.start()
        load_tiles = pltpu.make_async_copy(tile_hbm, at.tiles_v.at[core], local_sem.at[6])
        load_tiles.start()
        parts = [
            ("diag0", diag_hbm.at[:, low], diag32.at[core, :, low]),
            ("off0", off_hbm.at[low_p], off32.at[low_p, mine, :]),
            ("off1", off_hbm.at[high_p], off32.at[high_p, mine, :]),
            ("diag1", diag_hbm.at[:, high], diag32.at[core, :, high]),
        ]
        own_copies = {}
        for place, (name, source, target) in enumerate(parts):
            own_copies[name] = pltpu.make_async_copy(source, target, local_sem.at[place])
            own_copies[name].start()

        barrier = pltpu.get_barrier_semaphore()

        def greet_column(step, carry):
            _, device = column_peer(step)
            pl.semaphore_signal(barrier, inc=1, device_id=device, device_id_type=MESH)
            return carry

        def greet_plane(step, carry):
            _, device = plane_peer(chips, step)
            pl.semaphore_signal(barrier, inc=1, device_id=device, device_id_type=MESH)
            return carry

        lax.fori_loop(0, slots - 1, greet_column, 0)
        lax.fori_loop(0, chips - 1, greet_plane, 0)

        used = levels * chunk
        load_side.wait()
        side = at.side32[...].reshape(used, slots * group)
        side = jnp.concatenate([side, jnp.zeros((LANES - used, slots * group), jnp.float32)], axis=0)
        at.side_out[...] = side.T.reshape(slots, group, LANES)
        for level in range(1, levels):
            at.acc[level][...] = jnp.zeros_like(at.acc[level])
        at.w[...] = jnp.zeros_like(at.w)

        pl.semaphore_wait(barrier, slots - 1 + chips - 1)

        def send_side(step, carry):
            index, device = column_peer(step)
            send("side", at.side_out.at[index], at.side_in.at[own_rows], device)
            return carry

        partner = (2 * chip + 1 - core, z)
        send("tiles", tile_hbm, at.tiles_v.at[core], partner)
        lax.fori_loop(0, slots - 1, send_side, 0)
        for name, source, target in parts:
            send(name, source, target, partner)
        load_tiles.wait()
        own_copies["off1"].wait()
        group_chips = 2 ** (MIX_TOP - 1)
        in_group = lax.rem(chip, group_chips)
        at.ptiles_v[in_group] = at.tiles_v[core]

        def send_tiles(step, carry):
            _, device = plane_peer(group_chips, step)
            send("ptiles", at.tiles_v.at[core], at.ptiles_v.at[in_group], device)
            return carry

        lax.fori_loop(0, group_chips - 1, send_tiles, 0)
        share = pl.ds(pl.multiple_of(core * rows + z * chunk, chunk), chunk)

        def send_rows(level):
            count = 2 ** (level - 1)
            place = lax.rem(chip, count)
            rows_of = at.lrow[level]
            p = pair_slot(level - 1, level)
            rows_of[place] = off32[p, share, :]

            def one(step, carry):
                _, device = plane_peer(count, step)
                send(("lrow", level), off32.at[p, share, :], rows_of.at[place], device)
                return carry

            lax.fori_loop(0, count - 1, one, 0)

        for level in range(MIX_TOP, ONE_STEP, -1):
            send_rows(level)
        at.side_in[own_rows] = at.side_out[own_rhs]

        other = pl.ds(pl.multiple_of((1 - core) * rows, rows), rows)
        theirs = {
            "diag0": diag32.at[1 - core, :, low],
            "off0": off32.at[low_p, other, :],
            "off1": off32.at[high_p, other, :],
            "diag1": diag32.at[1 - core, :, high],
        }

        def arrived(name):
            if name != "off1":
                own_copies[name].wait()
            received(name, theirs[name])

        def put_diag(half, place, value):
            value_high, value_low = split(value)
            spot = pl.ds(half * rows, rows)
            at.diag_high[spot, place] = value_high
            at.diag_low[spot, place] = value_low

        wide_lane = lax.broadcasted_iota(jnp.int32, (rows, LANES), 1)

        def convert_diag(first, last):
            def block(j, carry):
                here = pl.ds(pl.multiple_of(j * LANES, LANES), LANES)
                before = pl.ds(pl.multiple_of((j - 1) * LANES, LANES), LANES)
                for half in range(2):
                    mixed = jnp.where(wide_lane < rows, diag32[half, :, here], diag32[half, :, before])
                    put_diag(half, here, pltpu.roll(mixed, rows, 1))
                return carry

            lax.fori_loop(first, last, block, 0)

        def copy_blocks(level):
            start = rows * 2**level

            def block(j, carry):
                here = pl.ds(pl.multiple_of(start + j * LANES, LANES), LANES)
                at.block_high[level][j] = at.diag_high[:, here]
                at.block_low[level][j] = at.diag_low[:, here]
                return carry

            lax.fori_loop(0, 2 ** (level - 1), block, 0)

        def convert_last_diag():
            j = cols // LANES
            for half in range(2):
                tail = diag32[half, :, j * LANES : cols]
                tail = jnp.concatenate([tail, jnp.zeros((rows, LANES - rows), jnp.float32)], axis=1)
                mixed = jnp.where(wide_lane < rows, tail, diag32[half, :, (j - 1) * LANES : j * LANES])
                put_diag(half, pl.ds(j * LANES, LANES), pltpu.roll(mixed, rows, 1))

        def convert_off(first, last):
            def block(p, carry):
                value_high, value_low = split(off32[p])
                at.off_high[p] = value_high
                at.off_low[p] = value_low
                return carry

            lax.fori_loop(first, last, block, 0)

        arrived("diag0")
        for half in range(2):
            first = jnp.where(wide_lane < rows, diag32[half, :, 0:LANES], 0.0)
            put_diag(half, pl.ds(0, LANES), first if half == 0 else pltpu.roll(first, rows, 1))
        convert_diag(1, low_cols // LANES)
        arrived("off0")
        convert_off(0, low_pairs)
        received("tiles", at.tiles_v.at[1 - core])
        to_smem = pltpu.make_async_copy(at.tiles_v, at.tiles_s, local_sem.at[4])
        to_smem.start()
        to_smem.wait()
        tiles = at.tiles_s

        received("side", at.side_in.at[pl.ds(0, slots - 1)])
        turned = []
        for s in range(slots):
            value = at.side_in[s]
            turned.append(pltpu.roll(value, s * chunk, 1) if s else value)
        for level in range(levels):
            value = turned[0]
            for s in range(1, slots):
                value = jnp.where(lane_block == (s + level) % slots, turned[s], value)
            at.b[level] = pltpu.roll(value, LANES - level * chunk, 1) if level else value

        def diag_block(level):
            if level == 0:
                place = pl.ds(0, LANES)
            else:
                place = pl.ds(rows * 2**level, rows * 2**level)
            return at.diag_high[:, place], at.diag_low[:, place]

        def contribute(source, level):
            p = pair_slot(source, level)
            known = at.y[source]
            stacked = jnp.concatenate([jnp.where(left_half, known, 0.0), jnp.where(left_half, 0.0, known)], axis=0)
            out = product(stacked, at.off_high[p], at.off_low[p], NN)
            pieces = []
            for half in range(2):
                for t in range(2):
                    piece = out[half * group : (half + 1) * group, t * LANES : (t + 1) * LANES]
                    pieces.append((piece, tiles[half, t, p]))
            acc = at.acc[level]
            count = 2 ** (level - 1)

            def add(target, carry):
                value = acc[target]
                for piece, number in pieces:
                    value = value - piece * (number == target).astype(jnp.float32)
                acc[target] = value
                return carry

            if count <= 4:
                for target in range(count):
                    add(target, 0)
            else:
                lax.fori_loop(0, count, add, 0)

        def gather_known(ancestor, level):
            p = pair_slot(level, ancestor)
            full = at.full[ancestor]
            halves = []
            for half in range(2):
                halves.append(jnp.concatenate([full[tiles[half, t, p]] for t in range(2)], axis=1))
            out = product(jnp.concatenate(halves, axis=0), at.off_high[p], at.off_low[p], NT)
            at.w[level] += jnp.where(left_half, out[:group], out[group:])

        def broadcast(name, source, level):
            count = 2 ** (level - 1)
            place = lax.rem(chip, count)
            target = table[name]

            def one(step, carry):
                _, device = plane_peer(count, step)
                send(name, source, target.at[place], device)
                return carry

            lax.fori_loop(0, count - 1, one, 0)

        def scatter(name, source, level):
            count = 2 ** (level - 1)
            place = lax.rem(chip, count)
            target = table[name]

            def one(step, carry):
                index, device = plane_peer(count, step)
                send(name, source.at[index], target.at[place], device)
                return carry

            lax.fori_loop(0, count - 1, one, 0)

        def await_all(name, level):
            count = 2 ** (level - 1)
            received(name, table[name].at[pl.ds(0, count - 1)])

        def total(ref, count):
            value = ref[0]
            for place in range(1, count):
                value = value + ref[place]
            return value

        def build_mix(level):
            count = 2 ** (level - 1)
            first_chip = in_group - lax.rem(chip, count)
            p = pair_slot(level - 1, level)
            rows_of, mix, numbers = at.lrow[level], at.mix[level], at.ptiles_s
            block_high, block_low = at.block_high[level], at.block_low[level]
            copy_blocks(level)

            def one(index, carry):
                value = rows_of[index]
                high_part = value.astype(jnp.bfloat16).astype(jnp.float32)
                both = jnp.concatenate([high_part, value - high_part], axis=0).astype(jnp.bfloat16)
                out = jnp.zeros((2 * chunk, LANES), jnp.float32)
                rest = jnp.zeros((2 * chunk, LANES), jnp.float32)
                for t in range(2):
                    number = numbers[first_chip + index, t, p]
                    piece = both[:, t * LANES : (t + 1) * LANES]
                    out += lax.dot_general(piece, block_high[number], NT, preferred_element_type=jnp.float32)
                    rest += lax.dot_general(piece, block_low[number], NT, preferred_element_type=jnp.float32)
                mix[index, own_rows] = out[:chunk] + out[chunk:] + rest[:chunk]
                return carry

            lax.fori_loop(0, count, one, 0)

            def give(step, carry):
                their_z = lax.rem(z + outward(step, grid), grid)
                part = mix.at[:, own_rows]
                send(("mix", level), part, part, (leaf, their_z))
                return carry

            lax.fori_loop(0, grid - 1, give, 0)

        def swap_mix(level):
            mix = at.mix[level]
            received(("mix", level), mix.at[:, pl.ds(0, grid - 1)])
            half = mix.at[:, pl.ds(core * grid, grid)]
            send(("swap", level), half, half, partner)

        def finish_mix(level):
            count = 2 ** (level - 1)
            mix = at.mix[level]
            received(("swap", level), mix.at[:, pl.ds((1 - core) * grid, grid)])

            def one(index, carry):
                value_high, value_low = split(mix[index].reshape(LANES, LANES))
                spot = pl.ds(pl.multiple_of(index * LANES, LANES), LANES)
                at.mix_high[level][spot, :] = value_high
                at.mix_low[level][spot, :] = value_low
                return carry

            lax.fori_loop(0, count, one, 0)

        at.y[0] = product(at.b[0], *diag_block(0), NT)
        contribute(0, 1)
        at.y[1] = product(at.b[1] + at.acc[1][0], *diag_block(1), NT)
        contribute(0, 2)
        def start_sums(level):
            count = 2 ** (level - 1)
            place = lax.rem(chip, count)
            acc, up = at.acc[level], at.up[level]
            if level <= ONE_STEP:
                acc[place] += at.b[level]
                broadcast(("up", level), acc, level)
                up[place] = acc[...]
            else:
                scatter(("up", level), acc, level)
                up[place] = acc[place]

        def spread_sum(level):
            count = 2 ** (level - 1)
            place = lax.rem(chip, count)
            await_all(("up", level), level)
            summed = at.sum[level]
            summed[place] = at.b[level] + total(at.up[level], count)
            broadcast(("sum", level), summed.at[place], level)

        def side_by_side(value, count):
            return jnp.concatenate([value[t] for t in range(count)], axis=1)

        def solve_level(level):
            count = 2 ** (level - 1)
            if level <= ONE_STEP:
                await_all(("up", level), level)
                whole = total(at.up[level], count)
            else:
                await_all(("sum", level), level)
                whole = at.sum[level][...]
            return product(side_by_side(whole, count), *diag_block(level), NT)

        contribute(1, 2)
        start_sums(2)
        contribute(0, 3)
        contribute(1, 3)
        arrived("off1")
        convert_off(low_pairs, pairs)
        at.y[2] = solve_level(2)
        contribute(2, 3)
        start_sums(3)
        for source in range(3):
            contribute(source, 4)
        arrived("diag1")
        convert_diag(low_cols // LANES, rows * 2 ** (MIX_TOP + 1) // LANES)
        received("ptiles", at.ptiles_v.at[pl.ds(0, group_chips - 1)])
        for upper in range(ONE_STEP + 1, MIX_TOP + 1):
            await_all(("lrow", upper), upper)
        numbers = pltpu.make_async_copy(at.ptiles_v, at.ptiles_s, local_sem.at[7])
        numbers.start()
        numbers.wait()
        build_mix(MIX_TOP)
        at.y[3] = solve_level(3)
        contribute(3, 4)
        start_sums(4)
        for source in range(4):
            contribute(source, MIX_TOP)
        start_sums(MIX_TOP)
        spread_sum(4)
        build_mix(4)
        spread_sum(MIX_TOP)
        at.y[4] = solve_level(4)
        count = 2 ** (MIX_TOP - 1)
        new = at.new[MIX_TOP]
        place = lax.rem(chip, count)
        new[place] = at.y[4]
        broadcast(("new", MIX_TOP), new.at[place], MIX_TOP)
        swap_mix(MIX_TOP)
        known = solve_level(MIX_TOP)
        for source in range(MIX_TOP):
            contribute(source, top)
        finish_mix(MIX_TOP)
        await_all(("new", MIX_TOP), MIX_TOP)
        at.y[MIX_TOP] = known - product(
            side_by_side(new[...], count), at.mix_high[MIX_TOP][...], at.mix_low[MIX_TOP][...], NN
        )
        contribute(MIX_TOP, top)
        start_sums(top)
        convert_diag(rows * 2**top // LANES, cols // LANES)
        convert_last_diag()
        spread_sum(top)
        swap_mix(4)
        finish_mix(4)
        at.y[top] = solve_level(top)

        def pack(values, name, outbox, inbox):
            turned = []
            for level in range(levels):
                value = values[level]
                turned.append(pltpu.roll(value, level * chunk, 1) if level else value)
            for s in range(slots):
                value = turned[0]
                for level in range(1, levels):
                    value = jnp.where(lane_block == (s + level) % slots, turned[level], value)
                outbox[s] = pltpu.roll(value, LANES - s * chunk, 1) if s else value

            def one(step, carry):
                index, device = row_peer(step)
                send(name, outbox.at[index], inbox.at[own_rhs], device)
                return carry

            lax.fori_loop(0, slots - 1, one, 0)
            inbox[own_rhs] = outbox[own_rows]

        def unpack(name, inbox, target):
            received(name, inbox.at[pl.ds(0, slots - 1)])
            value = inbox[...].reshape(slots * group, LANES).T
            for level in range(levels):
                target[level] = value[level * chunk : (level + 1) * chunk]

        def start_level(level):
            count = 2 ** (level - 1)
            place = lax.rem(chip, count)
            residue = at.y[level] - at.w[level]
            part, down = at.part[level], at.down[level]
            value = product(residue, *diag_block(level), NN)
            for t in range(count):
                part[t] = value[:, t * LANES : (t + 1) * LANES]
            if level <= ONE_STEP:
                broadcast(("down", level), part, level)
                down[place] = part[...]
                return
            if level > MIX_TOP:
                scatter(("down", level), part, level)
                down[place] = part[place]
                return
            mpart, mid = at.mpart[level], at.mid[level]
            value = product(residue, at.mix_high[level][...], at.mix_low[level][...], NT)
            for t in range(count):
                mpart[t] = value[:, t * LANES : (t + 1) * LANES]
            scatter(("mid", level), mpart, level)
            mid[place] = mpart[place]
            scatter(("down", level), part, level)
            down[place] = part[place]

        def spread_x(level):
            count = 2 ** (level - 1)
            place = lax.rem(chip, count)
            await_all(("down", level), level)
            value = total(at.down[level], count)
            at.x[level] = value
            at.full[level][place] = value
            broadcast(("full", level), at.full[level].at[place], level)

        def through_mix(level):
            await_all(("mid", level), level)
            at.w[level - 1] += total(at.mid[level], 2 ** (level - 1))

        def whole_x(level):
            count = 2 ** (level - 1)
            await_all(("down", level), level)
            at.full[level][...] = total(at.down[level], count)
            at.x[level] = at.full[level][lax.rem(chip, count)]

        start_level(top)
        pack(at.y, "fwd", at.fwd_out, at.fwd_in)
        spread_x(top)
        await_all(("full", top), top)
        gather_known(top, MIX_TOP)
        start_level(MIX_TOP)
        gather_known(top, MIX_TOP - 1)
        through_mix(MIX_TOP)
        start_level(ONE_STEP + 1)
        for below in range(ONE_STEP, -1, -1):
            gather_known(top, below)
        spread_x(MIX_TOP)
        through_mix(ONE_STEP + 1)
        await_all(("full", MIX_TOP), MIX_TOP)
        gather_known(MIX_TOP, ONE_STEP)
        start_level(ONE_STEP)
        spread_x(ONE_STEP + 1)
        for below in range(ONE_STEP - 1, -1, -1):
            gather_known(ONE_STEP + 2, below)
        unpack("fwd", at.fwd_in, fwd_ref)
        whole_x(ONE_STEP)
        await_all(("full", ONE_STEP + 1), ONE_STEP + 1)
        for below in range(ONE_STEP - 1, -1, -1):
            gather_known(ONE_STEP + 1, below)
        gather_known(ONE_STEP, ONE_STEP - 1)
        start_level(2)
        for below in (1, 0):
            gather_known(ONE_STEP, below)
        whole_x(2)
        gather_known(2, 1)
        value = product(at.y[1] - at.w[1], *diag_block(1), NN)
        at.x[1] = value
        at.full[1][0] = value
        gather_known(2, 0)
        gather_known(1, 0)
        at.x[0] = product(at.y[0] - at.w[0], *diag_block(0), NN)
        pack(at.x, "sol", at.sol_out, at.sol_in)
        unpack("sol", at.sol_in, sol_ref)
        for name, view in sent:
            await_bytes(view, send_sem.at[slot_of[name]])

    return kernel


def solution(mesh):
    grid = mesh.shape["grid"]

    def local(right_side, diag_inv, off_diag, tile_rows):
        levels, rhs, chunk = right_side.shape
        rows, cols = diag_inv.shape
        pairs = off_diag.shape[0]
        slots = 2 * grid
        group = rhs // slots
        side = jnp.transpose(right_side, (0, 2, 1))
        off = jnp.transpose(off_diag, (0, 2, 1))
        tiles = jnp.transpose(tile_rows[:, :, 0], (1, 0))
        plan, moves = scratch_plan(levels, pairs, rows, cols, group, slots)
        vmem = pl.BlockSpec(memory_space=pltpu.VMEM)
        hbm = pl.BlockSpec(memory_space=pltpu.HBM)
        out = jax.ShapeDtypeStruct(side.shape, jnp.float32)
        forward, backward = pl.pallas_call(
            make_kernel(levels, list(plan), moves, rows, cols, group, grid),
            out_shape=(out, out),
            in_specs=[hbm, hbm, hbm, hbm],
            out_specs=(vmem, vmem),
            scratch_shapes=list(plan.values()),
            compiler_params=pltpu.CompilerParams(
                collective_id=0, has_side_effects=True, vmem_limit_bytes=48 * 2**20
            ),
            name="tree_solve",
        )(*(pltpu.with_memory_space_constraint(part, pltpu.HBM) for part in (side, diag_inv, off, tiles)))
        return jnp.transpose(forward, (0, 2, 1)), jnp.transpose(backward, (0, 2, 1))

    in_specs = (
        P(None, None, ("leaf", "grid")),
        P("leaf", None),
        P(None, None, "leaf"),
        P(None, None, "leaf"),
    )
    out_specs = (P(None, None, ("leaf", "grid")), P(None, None, ("leaf", "grid")))
    return jax.shard_map(local, mesh=mesh, in_specs=in_specs, out_specs=out_specs, check_vma=False)
```

```python
import types

import jax
import jax.numpy as jnp
from jax import lax
from jax.experimental import pallas as pl
from jax.experimental.pallas import tpu as pltpu
from jax.sharding import PartitionSpec as P

MESH = pl.DeviceIdType.MESH
LANES = 128
ONE_STEP = 3
MIX_TOP = 5
NN = (((1,), (0,)), ((), ()))
NT = (((1,), (1,)), ((), ()))


def pair_slot(source, ancestor):
    return ancestor * (ancestor - 1) // 2 + source


def outward(place, size):
    away = (place + 1) // 2
    return lax.rem(size // 2 + away * (1 - 2 * lax.rem(place, 2)) + size, size)


def split(value):
    high = value.astype(jnp.bfloat16)
    low = (value - high.astype(jnp.float32)).astype(jnp.bfloat16)
    return high, low


def product(value, high, low, dims):
    rows = value.shape[0]
    value_high, value_low = split(value)
    both = lax.dot_general(
        jnp.concatenate([value_high, value_low], axis=0), high, dims, preferred_element_type=jnp.float32
    )
    rest = lax.dot_general(value_high, low, dims, preferred_element_type=jnp.float32)
    return both[:rows] + both[rows:] + rest


def scratch_plan(levels, pairs, rows, cols, group, slots):
    f32, bf16 = jnp.float32, jnp.bfloat16
    tile = (group, LANES)
    plan = {
        ("diag32", 0): pltpu.VMEM((2, rows, cols), f32),
        ("off32", 0): pltpu.VMEM((pairs, 2 * rows, 2 * LANES), f32),
        ("diag_high", 0): pltpu.VMEM((2 * rows, rows * 2**levels), bf16),
        ("diag_low", 0): pltpu.VMEM((2 * rows, rows * 2**levels), bf16),
        ("off_high", 0): pltpu.VMEM((pairs, 2 * rows, 2 * LANES), bf16),
        ("off_low", 0): pltpu.VMEM((pairs, 2 * rows, 2 * LANES), bf16),
        ("tiles_v", 0): pltpu.VMEM((2, 2, pairs), jnp.int32),
        ("tiles_s", 0): pltpu.SMEM((2, 2, pairs), jnp.int32),
    }
    plan["side32", 0] = pltpu.VMEM((levels, rows // (slots // 2), slots * group), f32)
    for name in ("side", "fwd", "sol"):
        plan[name + "_out", 0] = pltpu.VMEM((slots, group // 2, LANES), f32)
        plan[name + "_in", 0] = pltpu.VMEM((slots, group // 2, LANES), f32)
    for name in ("b", "y", "w", "x"):
        plan[name, 0] = pltpu.VMEM((levels,) + tile, f32)
    moves = ["side", "fwd", "sol", "diag0", "diag1", "off0", "off1", "tiles", "ptiles"]
    plan["ptiles_v", 0] = pltpu.VMEM((2 ** (MIX_TOP - 1), 2, pairs), jnp.int32)
    plan["ptiles_s", 0] = pltpu.SMEM((2 ** (MIX_TOP - 1), 2, pairs), jnp.int32)
    for level in range(1, levels):
        count = 2 ** (level - 1)
        plan["acc", level] = pltpu.VMEM((count,) + tile, f32)
        plan["full", level] = pltpu.VMEM((count,) + tile, f32)
        if level < 2:
            continue
        plan["part", level] = pltpu.VMEM((count,) + tile, f32)
        if level <= ONE_STEP:
            plan["up", level] = pltpu.VMEM((count, count) + tile, f32)
            plan["down", level] = pltpu.VMEM((count, count) + tile, f32)
            moves += [("up", level), ("down", level)]
        else:
            plan["up", level] = pltpu.VMEM((count,) + tile, f32)
            plan["down", level] = pltpu.VMEM((count,) + tile, f32)
            plan["sum", level] = pltpu.VMEM((count,) + tile, f32)
            moves += [("up", level), ("down", level), ("sum", level), ("full", level)]
            if level > MIX_TOP:
                continue
            plan["mid", level] = pltpu.VMEM((count,) + tile, f32)
            plan["mpart", level] = pltpu.VMEM((count,) + tile, f32)
            plan["lrow", level] = pltpu.VMEM((count, 2 * rows // slots, 2 * LANES), f32)
            plan["mix", level] = pltpu.VMEM((count, slots, 2 * rows // slots, LANES), f32)
            plan["block_high", level] = pltpu.VMEM((count, LANES, LANES), bf16)
            plan["block_low", level] = pltpu.VMEM((count, LANES, LANES), bf16)
            plan["mix_high", level] = pltpu.VMEM((count * LANES, LANES), bf16)
            plan["mix_low", level] = pltpu.VMEM((count * LANES, LANES), bf16)
            moves += [("mid", level), ("lrow", level), ("mix", level), ("swap", level)]
            if level == MIX_TOP:
                plan["new", level] = pltpu.VMEM((count,) + tile, f32)
                moves.append(("new", level))
    plan["send_sem", 0] = pltpu.SemaphoreType.DMA((len(moves),))
    plan["recv_sem", 0] = pltpu.SemaphoreType.DMA((len(moves),))
    plan["local_sem", 0] = pltpu.SemaphoreType.DMA((8,))
    return plan, moves


def make_kernel(levels, names, moves, rows, cols, group, grid):
    chunk = rows // grid
    slots = 2 * grid
    top = levels - 1
    chips = 2 ** (top - 1)
    low_cols = 1024
    low_pairs = 6
    ring = min(8, chips)

    def kernel(side_hbm, diag_hbm, off_hbm, tile_hbm, fwd_ref, sol_ref, *scratch):
        table = dict(zip(names, scratch))
        at = types.SimpleNamespace()
        for (name, level), ref in table.items():
            if level:
                vars(at).setdefault(name, {})[level] = ref
            else:
                vars(at)[name] = ref
        send_sem, recv_sem, local_sem = at.send_sem, at.recv_sem, at.local_sem
        slot_of = {name: place for place, name in enumerate(moves)}
        leaf, z = lax.axis_index("leaf"), lax.axis_index("grid")
        core = lax.rem(leaf, 2)
        chip = leaf // 2
        lane = lax.broadcasted_iota(jnp.int32, (group, LANES), 1)
        lane_block = lane // chunk
        left_half = lane < rows
        own_rhs = 2 * z + core
        own_rows = core * grid + z

        def column_device(step):
            their_z = lax.rem(z + outward(step // 2, grid), grid)
            their_core = lax.rem(core + 1 + lax.rem(step, 2), 2)
            return their_core, their_z, (2 * chip + their_core, their_z)

        def column_peer(step):
            their_core, their_z, device = column_device(step)
            return 2 * their_z + their_core, device

        def row_peer(step):
            their_core, their_z, device = column_device(step)
            return their_core * grid + their_z, device

        def plane_peer(count, step):
            place = lax.rem(chip, count)
            if count < ring:
                index = lax.rem(place + outward(step, count), count)
            else:
                lines = count // ring
                line = lax.rem(place // ring + outward(step // ring, lines), lines)
                index = line * ring + lax.rem(place + ring + (1 - 2 * core) * outward(lax.rem(step, ring), ring), ring)
            return index, (2 * (chip - place + index) + core, z)

        fold_rows = group // 2

        def fold(value):
            axis = value.ndim - 1
            lanes = lax.broadcasted_iota(jnp.int32, value.shape[:-2] + (fold_rows, LANES), axis)
            upper, lower = value[..., :fold_rows, :], value[..., fold_rows:, :]
            return jnp.where(lanes < LANES // 2, upper, pltpu.roll(lower, LANES // 2, axis))

        def unfold(value):
            axis = value.ndim - 1
            return jnp.concatenate([value, pltpu.roll(value, LANES // 2, axis)], axis=axis - 1)

        def send(name, source, target, device):
            pltpu.make_async_remote_copy(
                src_ref=source,
                dst_ref=target,
                send_sem=send_sem.at[slot_of[name]],
                recv_sem=recv_sem.at[slot_of[name]],
                device_id=device,
                device_id_type=MESH,
            ).start()

        def await_bytes(view, sem):
            pltpu.make_async_copy(view, view, sem).wait()

        sent = []

        def received(name, view):
            await_bytes(view, recv_sem.at[slot_of[name]])
            sent.append((name, view))

        diag32, off32 = at.diag32, at.off32
        low = pl.ds(0, low_cols)
        high = pl.ds(low_cols, cols - low_cols)
        mine = pl.ds(pl.multiple_of(core * rows, rows), rows)
        pairs = off_hbm.shape[0]
        low_p, high_p = pl.ds(0, low_pairs), pl.ds(low_pairs, pairs - low_pairs)
        load_side = pltpu.make_async_copy(side_hbm, at.side32, local_sem.at[5])
        load_side.start()
        load_tiles = pltpu.make_async_copy(tile_hbm, at.tiles_v.at[core], local_sem.at[6])
        load_tiles.start()
        parts = [
            ("diag0", diag_hbm.at[:, low], diag32.at[core, :, low]),
            ("off0", off_hbm.at[low_p], off32.at[low_p, mine, :]),
            ("off1", off_hbm.at[high_p], off32.at[high_p, mine, :]),
            ("diag1", diag_hbm.at[:, high], diag32.at[core, :, high]),
        ]
        own_copies = {}
        for place, (name, source, target) in enumerate(parts):
            own_copies[name] = pltpu.make_async_copy(source, target, local_sem.at[place])
            own_copies[name].start()

        barrier = pltpu.get_barrier_semaphore()

        def greet_column(step, carry):
            _, device = column_peer(step)
            pl.semaphore_signal(barrier, inc=1, device_id=device, device_id_type=MESH)
            return carry

        def greet_plane(step, carry):
            _, device = plane_peer(chips, step)
            pl.semaphore_signal(barrier, inc=1, device_id=device, device_id_type=MESH)
            return carry

        lax.fori_loop(0, chips - 1, greet_plane, 0)
        lax.fori_loop(0, slots - 1, greet_column, 0)

        used = levels * chunk
        load_side.wait()
        side = at.side32[...].reshape(used, slots * group)
        side = jnp.concatenate([side, jnp.zeros((LANES - used, slots * group), jnp.float32)], axis=0)
        at.side_out[...] = fold(side.T.reshape(slots, group, LANES))
        for level in range(1, levels):
            at.acc[level][...] = jnp.zeros_like(at.acc[level])
        at.w[...] = jnp.zeros_like(at.w)

        pl.semaphore_wait(barrier, slots - 1 + chips - 1)

        def send_side(step, carry):
            index, device = column_peer(step)
            send("side", at.side_out.at[index], at.side_in.at[own_rows], device)
            return carry

        partner = (2 * chip + 1 - core, z)
        send("tiles", tile_hbm, at.tiles_v.at[core], partner)
        lax.fori_loop(0, slots - 1, send_side, 0)
        for name, source, target in parts:
            send(name, source, target, partner)
        load_tiles.wait()
        own_copies["off1"].wait()
        group_chips = 2 ** (MIX_TOP - 1)
        in_group = lax.rem(chip, group_chips)
        at.ptiles_v[in_group] = at.tiles_v[core]

        def send_tiles(step, carry):
            _, device = plane_peer(group_chips, step)
            send("ptiles", at.tiles_v.at[core], at.ptiles_v.at[in_group], device)
            return carry

        lax.fori_loop(0, group_chips - 1, send_tiles, 0)
        share = pl.ds(pl.multiple_of(core * rows + z * chunk, chunk), chunk)

        def send_rows(level):
            count = 2 ** (level - 1)
            place = lax.rem(chip, count)
            rows_of = at.lrow[level]
            p = pair_slot(level - 1, level)
            rows_of[place] = off32[p, share, :]

            def one(step, carry):
                _, device = plane_peer(count, step)
                send(("lrow", level), off32.at[p, share, :], rows_of.at[place], device)
                return carry

            lax.fori_loop(0, count - 1, one, 0)

        for level in range(MIX_TOP, ONE_STEP, -1):
            send_rows(level)
        at.side_in[own_rows] = at.side_out[own_rhs]

        other = pl.ds(pl.multiple_of((1 - core) * rows, rows), rows)
        theirs = {
            "diag0": diag32.at[1 - core, :, low],
            "off0": off32.at[low_p, other, :],
            "off1": off32.at[high_p, other, :],
            "diag1": diag32.at[1 - core, :, high],
        }

        def arrived(name):
            if name != "off1":
                own_copies[name].wait()
            received(name, theirs[name])

        def put_diag(half, place, value):
            value_high, value_low = split(value)
            spot = pl.ds(half * rows, rows)
            at.diag_high[spot, place] = value_high
            at.diag_low[spot, place] = value_low

        wide_lane = lax.broadcasted_iota(jnp.int32, (rows, LANES), 1)

        def convert_diag(first, last):
            def block(j, carry):
                here = pl.ds(pl.multiple_of(j * LANES, LANES), LANES)
                before = pl.ds(pl.multiple_of((j - 1) * LANES, LANES), LANES)
                for half in range(2):
                    mixed = jnp.where(wide_lane < rows, diag32[half, :, here], diag32[half, :, before])
                    put_diag(half, here, pltpu.roll(mixed, rows, 1))
                return carry

            lax.fori_loop(first, last, block, 0)

        def copy_blocks(level):
            start = rows * 2**level

            def block(j, carry):
                here = pl.ds(pl.multiple_of(start + j * LANES, LANES), LANES)
                at.block_high[level][j] = at.diag_high[:, here]
                at.block_low[level][j] = at.diag_low[:, here]
                return carry

            lax.fori_loop(0, 2 ** (level - 1), block, 0)

        def convert_last_diag():
            j = cols // LANES
            for half in range(2):
                tail = diag32[half, :, j * LANES : cols]
                tail = jnp.concatenate([tail, jnp.zeros((rows, LANES - rows), jnp.float32)], axis=1)
                mixed = jnp.where(wide_lane < rows, tail, diag32[half, :, (j - 1) * LANES : j * LANES])
                put_diag(half, pl.ds(j * LANES, LANES), pltpu.roll(mixed, rows, 1))

        def convert_off(first, last):
            def block(p, carry):
                value_high, value_low = split(off32[p])
                at.off_high[p] = value_high
                at.off_low[p] = value_low
                return carry

            lax.fori_loop(first, last, block, 0)

        arrived("diag0")
        for half in range(2):
            first = jnp.where(wide_lane < rows, diag32[half, :, 0:LANES], 0.0)
            put_diag(half, pl.ds(0, LANES), first if half == 0 else pltpu.roll(first, rows, 1))
        convert_diag(1, low_cols // LANES)
        arrived("off0")
        convert_off(0, low_pairs)
        received("tiles", at.tiles_v.at[1 - core])
        to_smem = pltpu.make_async_copy(at.tiles_v, at.tiles_s, local_sem.at[4])
        to_smem.start()
        to_smem.wait()
        tiles = at.tiles_s

        received("side", at.side_in.at[pl.ds(0, slots - 1)])
        turned = []
        for s in range(slots):
            value = unfold(at.side_in[s])
            turned.append(pltpu.roll(value, s * chunk, 1) if s else value)
        for level in range(levels):
            value = turned[0]
            for s in range(1, slots):
                value = jnp.where(lane_block == (s + level) % slots, turned[s], value)
            at.b[level] = pltpu.roll(value, LANES - level * chunk, 1) if level else value

        def diag_block(level):
            if level == 0:
                place = pl.ds(0, LANES)
            else:
                place = pl.ds(rows * 2**level, rows * 2**level)
            return at.diag_high[:, place], at.diag_low[:, place]

        def contribute(source, level):
            p = pair_slot(source, level)
            known = at.y[source]
            stacked = jnp.concatenate([jnp.where(left_half, known, 0.0), jnp.where(left_half, 0.0, known)], axis=0)
            out = product(stacked, at.off_high[p], at.off_low[p], NN)
            pieces = []
            for half in range(2):
                for t in range(2):
                    piece = out[half * group : (half + 1) * group, t * LANES : (t + 1) * LANES]
                    pieces.append((piece, tiles[half, t, p]))
            acc = at.acc[level]
            count = 2 ** (level - 1)

            def add(target, carry):
                value = acc[target]
                for piece, number in pieces:
                    value = value - piece * (number == target).astype(jnp.float32)
                acc[target] = value
                return carry

            if count <= 4:
                for target in range(count):
                    add(target, 0)
            else:
                lax.fori_loop(0, count, add, 0)

        def gather_known(ancestor, level):
            p = pair_slot(level, ancestor)
            full = at.full[ancestor]
            halves = []
            for half in range(2):
                halves.append(jnp.concatenate([full[tiles[half, t, p]] for t in range(2)], axis=1))
            out = product(jnp.concatenate(halves, axis=0), at.off_high[p], at.off_low[p], NT)
            at.w[level] += jnp.where(left_half, out[:group], out[group:])

        def broadcast(name, source, level):
            count = 2 ** (level - 1)
            place = lax.rem(chip, count)
            target = table[name]

            def one(step, carry):
                _, device = plane_peer(count, step)
                send(name, source, target.at[place], device)
                return carry

            lax.fori_loop(0, count - 1, one, 0)

        def scatter(name, source, level):
            count = 2 ** (level - 1)
            place = lax.rem(chip, count)
            target = table[name]

            def one(step, carry):
                index, device = plane_peer(count, step)
                send(name, source.at[index], target.at[place], device)
                return carry

            lax.fori_loop(0, count - 1, one, 0)

        def await_all(name, level):
            count = 2 ** (level - 1)
            received(name, table[name].at[pl.ds(0, count - 1)])

        def total(ref, count):
            value = ref[0]
            for place in range(1, count):
                value = value + ref[place]
            return value

        def build_mix(level):
            count = 2 ** (level - 1)
            first_chip = in_group - lax.rem(chip, count)
            p = pair_slot(level - 1, level)
            rows_of, mix, numbers = at.lrow[level], at.mix[level], at.ptiles_s
            block_high, block_low = at.block_high[level], at.block_low[level]
            copy_blocks(level)

            def one(index, carry):
                value = rows_of[index]
                high_part = value.astype(jnp.bfloat16).astype(jnp.float32)
                both = jnp.concatenate([high_part, value - high_part], axis=0).astype(jnp.bfloat16)
                out = jnp.zeros((2 * chunk, LANES), jnp.float32)
                rest = jnp.zeros((2 * chunk, LANES), jnp.float32)
                for t in range(2):
                    number = numbers[first_chip + index, t, p]
                    piece = both[:, t * LANES : (t + 1) * LANES]
                    out += lax.dot_general(piece, block_high[number], NT, preferred_element_type=jnp.float32)
                    rest += lax.dot_general(piece, block_low[number], NT, preferred_element_type=jnp.float32)
                mix[index, own_rows] = out[:chunk] + out[chunk:] + rest[:chunk]
                return carry

            lax.fori_loop(0, count, one, 0)

            def give(step, carry):
                their_z = lax.rem(z + outward(step, grid), grid)
                part = mix.at[:, own_rows]
                send(("mix", level), part, part, (leaf, their_z))
                return carry

            lax.fori_loop(0, grid - 1, give, 0)

        def swap_mix(level):
            mix = at.mix[level]
            received(("mix", level), mix.at[:, pl.ds(0, grid - 1)])
            half = mix.at[:, pl.ds(core * grid, grid)]
            send(("swap", level), half, half, partner)

        def finish_mix(level):
            count = 2 ** (level - 1)
            mix = at.mix[level]
            received(("swap", level), mix.at[:, pl.ds((1 - core) * grid, grid)])

            def one(index, carry):
                value_high, value_low = split(mix[index].reshape(LANES, LANES))
                spot = pl.ds(pl.multiple_of(index * LANES, LANES), LANES)
                at.mix_high[level][spot, :] = value_high
                at.mix_low[level][spot, :] = value_low
                return carry

            lax.fori_loop(0, count, one, 0)

        at.y[0] = product(at.b[0], *diag_block(0), NT)
        contribute(0, 1)
        at.y[1] = product(at.b[1] + at.acc[1][0], *diag_block(1), NT)
        contribute(0, 2)
        def start_sums(level):
            count = 2 ** (level - 1)
            place = lax.rem(chip, count)
            acc, up = at.acc[level], at.up[level]
            if level <= ONE_STEP:
                acc[place] += at.b[level]
                broadcast(("up", level), acc, level)
                up[place] = acc[...]
            else:
                scatter(("up", level), acc, level)
                up[place] = acc[place]

        def spread_sum(level):
            count = 2 ** (level - 1)
            place = lax.rem(chip, count)
            await_all(("up", level), level)
            summed = at.sum[level]
            summed[place] = at.b[level] + total(at.up[level], count)
            broadcast(("sum", level), summed.at[place], level)

        def side_by_side(value, count):
            return jnp.concatenate([value[t] for t in range(count)], axis=1)

        def solve_level(level):
            count = 2 ** (level - 1)
            if level <= ONE_STEP:
                await_all(("up", level), level)
                whole = total(at.up[level], count)
            else:
                await_all(("sum", level), level)
                whole = at.sum[level][...]
            return product(side_by_side(whole, count), *diag_block(level), NT)

        contribute(1, 2)
        start_sums(2)
        contribute(0, 3)
        contribute(1, 3)
        arrived("off1")
        convert_off(low_pairs, pairs)
        at.y[2] = solve_level(2)
        contribute(2, 3)
        start_sums(3)
        for source in range(3):
            contribute(source, 4)
        arrived("diag1")
        convert_diag(low_cols // LANES, rows * 2 ** (MIX_TOP + 1) // LANES)
        received("ptiles", at.ptiles_v.at[pl.ds(0, group_chips - 1)])
        for upper in range(ONE_STEP + 1, MIX_TOP + 1):
            await_all(("lrow", upper), upper)
        numbers = pltpu.make_async_copy(at.ptiles_v, at.ptiles_s, local_sem.at[7])
        numbers.start()
        numbers.wait()
        build_mix(MIX_TOP)
        at.y[3] = solve_level(3)
        contribute(3, 4)
        start_sums(4)
        for source in range(4):
            contribute(source, MIX_TOP)
        start_sums(MIX_TOP)
        spread_sum(4)
        build_mix(4)
        spread_sum(MIX_TOP)
        at.y[4] = solve_level(4)
        count = 2 ** (MIX_TOP - 1)
        new = at.new[MIX_TOP]
        place = lax.rem(chip, count)
        new[place] = at.y[4]
        broadcast(("new", MIX_TOP), new.at[place], MIX_TOP)
        swap_mix(MIX_TOP)
        known = solve_level(MIX_TOP)
        for source in range(MIX_TOP):
            contribute(source, top)
        finish_mix(MIX_TOP)
        await_all(("new", MIX_TOP), MIX_TOP)
        at.y[MIX_TOP] = known - product(
            side_by_side(new[...], count), at.mix_high[MIX_TOP][...], at.mix_low[MIX_TOP][...], NN
        )
        contribute(MIX_TOP, top)
        start_sums(top)
        convert_diag(rows * 2**top // LANES, cols // LANES)
        convert_last_diag()
        spread_sum(top)
        swap_mix(4)
        finish_mix(4)
        at.y[top] = solve_level(top)

        def pack(values, name, outbox, inbox):
            turned = []
            for level in range(levels):
                value = values[level]
                turned.append(pltpu.roll(value, level * chunk, 1) if level else value)
            for s in range(slots):
                value = turned[0]
                for level in range(1, levels):
                    value = jnp.where(lane_block == (s + level) % slots, turned[level], value)
                outbox[s] = fold(pltpu.roll(value, LANES - s * chunk, 1) if s else value)

            def one(step, carry):
                index, device = row_peer(step)
                send(name, outbox.at[index], inbox.at[own_rhs], device)
                return carry

            lax.fori_loop(0, slots - 1, one, 0)
            inbox[own_rhs] = outbox[own_rows]

        def unpack(name, inbox, target):
            received(name, inbox.at[pl.ds(0, slots - 1)])
            value = unfold(inbox[...]).reshape(slots * group, LANES).T
            for level in range(levels):
                target[level] = value[level * chunk : (level + 1) * chunk]

        def start_level(level):
            count = 2 ** (level - 1)
            place = lax.rem(chip, count)
            residue = at.y[level] - at.w[level]
            part, down = at.part[level], at.down[level]
            value = product(residue, *diag_block(level), NN)
            for t in range(count):
                part[t] = value[:, t * LANES : (t + 1) * LANES]
            if level <= ONE_STEP:
                broadcast(("down", level), part, level)
                down[place] = part[...]
                return
            if level > MIX_TOP:
                scatter(("down", level), part, level)
                down[place] = part[place]
                return
            mpart, mid = at.mpart[level], at.mid[level]
            value = product(residue, at.mix_high[level][...], at.mix_low[level][...], NT)
            for t in range(count):
                mpart[t] = value[:, t * LANES : (t + 1) * LANES]
            scatter(("mid", level), mpart, level)
            mid[place] = mpart[place]
            scatter(("down", level), part, level)
            down[place] = part[place]

        def spread_x(level):
            count = 2 ** (level - 1)
            place = lax.rem(chip, count)
            await_all(("down", level), level)
            value = total(at.down[level], count)
            at.x[level] = value
            at.full[level][place] = value
            broadcast(("full", level), at.full[level].at[place], level)

        def through_mix(level):
            await_all(("mid", level), level)
            at.w[level - 1] += total(at.mid[level], 2 ** (level - 1))

        def whole_x(level):
            count = 2 ** (level - 1)
            await_all(("down", level), level)
            at.full[level][...] = total(at.down[level], count)
            at.x[level] = at.full[level][lax.rem(chip, count)]

        start_level(top)
        pack(at.y, "fwd", at.fwd_out, at.fwd_in)
        spread_x(top)
        await_all(("full", top), top)
        gather_known(top, MIX_TOP)
        start_level(MIX_TOP)
        gather_known(top, MIX_TOP - 1)
        through_mix(MIX_TOP)
        start_level(ONE_STEP + 1)
        spread_x(MIX_TOP)
        for below in range(ONE_STEP, -1, -1):
            gather_known(top, below)
        through_mix(ONE_STEP + 1)
        await_all(("full", MIX_TOP), MIX_TOP)
        gather_known(MIX_TOP, ONE_STEP)
        start_level(ONE_STEP)
        spread_x(ONE_STEP + 1)
        for below in range(ONE_STEP - 1, -1, -1):
            gather_known(ONE_STEP + 2, below)
        unpack("fwd", at.fwd_in, fwd_ref)
        whole_x(ONE_STEP)
        await_all(("full", ONE_STEP + 1), ONE_STEP + 1)
        gather_known(ONE_STEP + 1, 2)
        gather_known(ONE_STEP, 2)
        start_level(2)
        for below in (1, 0):
            gather_known(ONE_STEP + 1, below)
            gather_known(ONE_STEP, below)
        whole_x(2)
        gather_known(2, 1)
        value = product(at.y[1] - at.w[1], *diag_block(1), NN)
        at.x[1] = value
        at.full[1][0] = value
        gather_known(2, 0)
        gather_known(1, 0)
        at.x[0] = product(at.y[0] - at.w[0], *diag_block(0), NN)
        pack(at.x, "sol", at.sol_out, at.sol_in)
        unpack("sol", at.sol_in, sol_ref)
        for name, view in sent:
            await_bytes(view, send_sem.at[slot_of[name]])

    return kernel


def solution(mesh):
    grid = mesh.shape["grid"]

    def local(right_side, diag_inv, off_diag, tile_rows):
        levels, rhs, chunk = right_side.shape
        rows, cols = diag_inv.shape
        pairs = off_diag.shape[0]
        slots = 2 * grid
        group = rhs // slots
        side = jnp.transpose(right_side, (0, 2, 1))
        off = jnp.transpose(off_diag, (0, 2, 1))
        tiles = jnp.transpose(tile_rows[:, :, 0], (1, 0))
        plan, moves = scratch_plan(levels, pairs, rows, cols, group, slots)
        vmem = pl.BlockSpec(memory_space=pltpu.VMEM)
        hbm = pl.BlockSpec(memory_space=pltpu.HBM)
        out = jax.ShapeDtypeStruct(side.shape, jnp.float32)
        forward, backward = pl.pallas_call(
            make_kernel(levels, list(plan), moves, rows, cols, group, grid),
            out_shape=(out, out),
            in_specs=[hbm, hbm, hbm, hbm],
            out_specs=(vmem, vmem),
            scratch_shapes=list(plan.values()),
            compiler_params=pltpu.CompilerParams(
                collective_id=0, has_side_effects=True, vmem_limit_bytes=48 * 2**20
            ),
            name="tree_solve",
        )(*(pltpu.with_memory_space_constraint(part, pltpu.HBM) for part in (side, diag_inv, off, tiles)))
        return jnp.transpose(forward, (0, 2, 1)), jnp.transpose(backward, (0, 2, 1))

    in_specs = (
        P(None, None, ("leaf", "grid")),
        P("leaf", None),
        P(None, None, "leaf"),
        P(None, None, "leaf"),
    )
    out_specs = (P(None, None, ("leaf", "grid")), P(None, None, ("leaf", "grid")))
    return jax.shard_map(local, mesh=mesh, in_specs=in_specs, out_specs=out_specs, check_vma=False)
```

```python
import types

import jax
import jax.numpy as jnp
from jax import lax
from jax.experimental import pallas as pl
from jax.experimental.pallas import tpu as pltpu
from jax.sharding import PartitionSpec as P

MESH = pl.DeviceIdType.MESH
LANES = 128
ONE_STEP = 3
MIX_TOP = 5
NN = (((1,), (0,)), ((), ()))
NT = (((1,), (1,)), ((), ()))


def pair_slot(source, ancestor):
    return ancestor * (ancestor - 1) // 2 + source


def outward(place, size):
    away = (place + 1) // 2
    return lax.rem(size // 2 + away * (1 - 2 * lax.rem(place, 2)) + size, size)


def split(value):
    high = value.astype(jnp.bfloat16)
    low = (value - high.astype(jnp.float32)).astype(jnp.bfloat16)
    return high, low


def product(value, high, low, dims):
    rows = value.shape[0]
    value_high, value_low = split(value)
    both = lax.dot_general(
        jnp.concatenate([value_high, value_low], axis=0), high, dims, preferred_element_type=jnp.float32
    )
    rest = lax.dot_general(value_high, low, dims, preferred_element_type=jnp.float32)
    return both[:rows] + both[rows:] + rest


def scratch_plan(levels, pairs, rows, cols, group, slots):
    f32, bf16 = jnp.float32, jnp.bfloat16
    tile = (group, LANES)
    plan = {
        ("diag32", 0): pltpu.VMEM((2, rows, cols), f32),
        ("off32", 0): pltpu.VMEM((pairs, 2 * rows, 2 * LANES), f32),
        ("diag_high", 0): pltpu.VMEM((2 * rows, rows * 2**levels), bf16),
        ("diag_low", 0): pltpu.VMEM((2 * rows, rows * 2**levels), bf16),
        ("off_high", 0): pltpu.VMEM((pairs, 2 * rows, 2 * LANES), bf16),
        ("off_low", 0): pltpu.VMEM((pairs, 2 * rows, 2 * LANES), bf16),
        ("tiles_v", 0): pltpu.VMEM((2, 2, pairs), jnp.int32),
        ("tiles_s", 0): pltpu.SMEM((2, 2, pairs), jnp.int32),
    }
    plan["side32", 0] = pltpu.VMEM((levels, rows // (slots // 2), slots * group), f32)
    for name in ("side", "fwd", "sol"):
        plan[name + "_out", 0] = pltpu.VMEM((slots, group // 2, LANES), f32)
        plan[name + "_in", 0] = pltpu.VMEM((slots, group // 2, LANES), f32)
    for name in ("b", "y", "w", "x"):
        plan[name, 0] = pltpu.VMEM((levels,) + tile, f32)
    moves = ["side", "fwd", "sol", "diag0", "diag1", "off0", "off1", "tiles", "ptiles"]
    plan["ptiles_v", 0] = pltpu.VMEM((2 ** (MIX_TOP - 1), 2, pairs), jnp.int32)
    plan["ptiles_s", 0] = pltpu.SMEM((2 ** (MIX_TOP - 1), 2, pairs), jnp.int32)
    for level in range(1, levels):
        count = 2 ** (level - 1)
        plan["acc", level] = pltpu.VMEM((count,) + tile, f32)
        plan["full", level] = pltpu.VMEM((count,) + tile, f32)
        if level < 2:
            continue
        plan["part", level] = pltpu.VMEM((count,) + tile, f32)
        if level <= ONE_STEP:
            plan["up", level] = pltpu.VMEM((count, count) + tile, f32)
            plan["down", level] = pltpu.VMEM((count, count) + tile, f32)
            moves += [("up", level), ("down", level)]
        else:
            plan["up", level] = pltpu.VMEM((count,) + tile, f32)
            plan["down", level] = pltpu.VMEM((count,) + tile, f32)
            plan["sum", level] = pltpu.VMEM((count,) + tile, f32)
            moves += [("up", level), ("down", level), ("sum", level), ("full", level)]
            if level > MIX_TOP:
                continue
            plan["mid", level] = pltpu.VMEM((count,) + tile, f32)
            plan["mpart", level] = pltpu.VMEM((count,) + tile, f32)
            plan["lrow", level] = pltpu.VMEM((count, 2 * rows // slots, 2 * LANES), f32)
            plan["mix", level] = pltpu.VMEM((count, slots, 2 * rows // slots, LANES), f32)
            plan["block_high", level] = pltpu.VMEM((count, LANES, LANES), bf16)
            plan["block_low", level] = pltpu.VMEM((count, LANES, LANES), bf16)
            plan["mix_high", level] = pltpu.VMEM((count * LANES, LANES), bf16)
            plan["mix_low", level] = pltpu.VMEM((count * LANES, LANES), bf16)
            moves += [("mid", level), ("lrow", level), ("mix", level), ("swap", level)]
            if level == MIX_TOP:
                plan["new", level] = pltpu.VMEM((count,) + tile, f32)
                moves.append(("new", level))
    plan["send_sem", 0] = pltpu.SemaphoreType.DMA((len(moves),))
    plan["recv_sem", 0] = pltpu.SemaphoreType.DMA((len(moves),))
    plan["local_sem", 0] = pltpu.SemaphoreType.DMA((8,))
    return plan, moves


def make_kernel(levels, names, moves, rows, cols, group, grid):
    chunk = rows // grid
    slots = 2 * grid
    top = levels - 1
    chips = 2 ** (top - 1)
    low_cols = 1024
    low_pairs = 6
    ring = min(8, chips)

    def kernel(side_hbm, diag_hbm, off_hbm, tile_hbm, fwd_ref, sol_ref, *scratch):
        table = dict(zip(names, scratch))
        at = types.SimpleNamespace()
        for (name, level), ref in table.items():
            if level:
                vars(at).setdefault(name, {})[level] = ref
            else:
                vars(at)[name] = ref
        send_sem, recv_sem, local_sem = at.send_sem, at.recv_sem, at.local_sem
        slot_of = {name: place for place, name in enumerate(moves)}
        leaf, z = lax.axis_index("leaf"), lax.axis_index("grid")
        core = lax.rem(leaf, 2)
        chip = leaf // 2
        lane = lax.broadcasted_iota(jnp.int32, (group, LANES), 1)
        lane_block = lane // chunk
        left_half = lane < rows
        own_rhs = 2 * z + core
        own_rows = core * grid + z

        def column_device(step):
            their_z = lax.rem(z + grid + (1 - 2 * core) * outward(step // 2, grid), grid)
            their_core = lax.rem(core + 1 + lax.rem(step, 2), 2)
            return their_core, their_z, (2 * chip + their_core, their_z)

        def column_peer(step):
            their_core, their_z, device = column_device(step)
            return 2 * their_z + their_core, device

        def row_peer(step):
            their_core, their_z, device = column_device(step)
            return their_core * grid + their_z, device

        def plane_peer(count, step):
            place = lax.rem(chip, count)
            if count < ring:
                index = lax.rem(place + outward(step, count), count)
            else:
                lines = count // ring
                line = lax.rem(place // ring + outward(step // ring, lines), lines)
                index = line * ring + lax.rem(place + ring + (1 - 2 * core) * outward(lax.rem(step, ring), ring), ring)
            return index, (2 * (chip - place + index) + core, z)

        fold_rows = group // 2

        def fold(value):
            axis = value.ndim - 1
            lanes = lax.broadcasted_iota(jnp.int32, value.shape[:-2] + (fold_rows, LANES), axis)
            upper, lower = value[..., :fold_rows, :], value[..., fold_rows:, :]
            return jnp.where(lanes < LANES // 2, upper, pltpu.roll(lower, LANES // 2, axis))

        def unfold(value):
            axis = value.ndim - 1
            return jnp.concatenate([value, pltpu.roll(value, LANES // 2, axis)], axis=axis - 1)

        def send(name, source, target, device):
            pltpu.make_async_remote_copy(
                src_ref=source,
                dst_ref=target,
                send_sem=send_sem.at[slot_of[name]],
                recv_sem=recv_sem.at[slot_of[name]],
                device_id=device,
                device_id_type=MESH,
            ).start()

        def await_bytes(view, sem):
            pltpu.make_async_copy(view, view, sem).wait()

        sent = []

        def received(name, view):
            await_bytes(view, recv_sem.at[slot_of[name]])
            sent.append((name, view))

        diag32, off32 = at.diag32, at.off32
        low = pl.ds(0, low_cols)
        high = pl.ds(low_cols, cols - low_cols)
        mine = pl.ds(pl.multiple_of(core * rows, rows), rows)
        pairs = off_hbm.shape[0]
        low_p, high_p = pl.ds(0, low_pairs), pl.ds(low_pairs, pairs - low_pairs)
        load_side = pltpu.make_async_copy(side_hbm, at.side32, local_sem.at[5])
        load_side.start()
        load_tiles = pltpu.make_async_copy(tile_hbm, at.tiles_v.at[core], local_sem.at[6])
        load_tiles.start()
        parts = [
            ("diag0", diag_hbm.at[:, low], diag32.at[core, :, low]),
            ("off0", off_hbm.at[low_p], off32.at[low_p, mine, :]),
            ("off1", off_hbm.at[high_p], off32.at[high_p, mine, :]),
            ("diag1", diag_hbm.at[:, high], diag32.at[core, :, high]),
        ]
        own_copies = {}
        for place, (name, source, target) in enumerate(parts):
            own_copies[name] = pltpu.make_async_copy(source, target, local_sem.at[place])
            own_copies[name].start()

        barrier = pltpu.get_barrier_semaphore()

        def greet_column(step, carry):
            _, device = column_peer(step)
            pl.semaphore_signal(barrier, inc=1, device_id=device, device_id_type=MESH)
            return carry

        def greet_plane(step, carry):
            _, device = plane_peer(chips, step)
            pl.semaphore_signal(barrier, inc=1, device_id=device, device_id_type=MESH)
            return carry

        lax.fori_loop(0, chips - 1, greet_plane, 0)
        lax.fori_loop(0, slots - 1, greet_column, 0)

        used = levels * chunk
        load_side.wait()
        side = at.side32[...].reshape(used, slots * group)
        side = jnp.concatenate([side, jnp.zeros((LANES - used, slots * group), jnp.float32)], axis=0)
        at.side_out[...] = fold(side.T.reshape(slots, group, LANES))
        for level in range(1, levels):
            at.acc[level][...] = jnp.zeros_like(at.acc[level])
        at.w[...] = jnp.zeros_like(at.w)

        pl.semaphore_wait(barrier, slots - 1 + chips - 1)

        def send_side(step, carry):
            index, device = column_peer(step)
            send("side", at.side_out.at[index], at.side_in.at[own_rows], device)
            return carry

        partner = (2 * chip + 1 - core, z)
        send("tiles", tile_hbm, at.tiles_v.at[core], partner)
        lax.fori_loop(0, slots - 1, send_side, 0)
        for name, source, target in parts:
            send(name, source, target, partner)
        load_tiles.wait()
        own_copies["off1"].wait()
        group_chips = 2 ** (MIX_TOP - 1)
        in_group = lax.rem(chip, group_chips)
        at.ptiles_v[in_group] = at.tiles_v[core]

        def send_tiles(step, carry):
            _, device = plane_peer(group_chips, step)
            send("ptiles", at.tiles_v.at[core], at.ptiles_v.at[in_group], device)
            return carry

        lax.fori_loop(0, group_chips - 1, send_tiles, 0)
        share = pl.ds(pl.multiple_of(core * rows + z * chunk, chunk), chunk)

        def send_rows(level):
            count = 2 ** (level - 1)
            place = lax.rem(chip, count)
            rows_of = at.lrow[level]
            p = pair_slot(level - 1, level)
            rows_of[place] = off32[p, share, :]

            def one(step, carry):
                _, device = plane_peer(count, step)
                send(("lrow", level), off32.at[p, share, :], rows_of.at[place], device)
                return carry

            lax.fori_loop(0, count - 1, one, 0)

        for level in range(MIX_TOP, ONE_STEP, -1):
            send_rows(level)
        at.side_in[own_rows] = at.side_out[own_rhs]

        other = pl.ds(pl.multiple_of((1 - core) * rows, rows), rows)
        theirs = {
            "diag0": diag32.at[1 - core, :, low],
            "off0": off32.at[low_p, other, :],
            "off1": off32.at[high_p, other, :],
            "diag1": diag32.at[1 - core, :, high],
        }

        def arrived(name):
            if name != "off1":
                own_copies[name].wait()
            received(name, theirs[name])

        def put_diag(half, place, value):
            value_high, value_low = split(value)
            spot = pl.ds(half * rows, rows)
            at.diag_high[spot, place] = value_high
            at.diag_low[spot, place] = value_low

        wide_lane = lax.broadcasted_iota(jnp.int32, (rows, LANES), 1)

        def convert_diag(first, last):
            def block(j, carry):
                here = pl.ds(pl.multiple_of(j * LANES, LANES), LANES)
                before = pl.ds(pl.multiple_of((j - 1) * LANES, LANES), LANES)
                for half in range(2):
                    mixed = jnp.where(wide_lane < rows, diag32[half, :, here], diag32[half, :, before])
                    put_diag(half, here, pltpu.roll(mixed, rows, 1))
                return carry

            lax.fori_loop(first, last, block, 0)

        def copy_blocks(level):
            start = rows * 2**level

            def block(j, carry):
                here = pl.ds(pl.multiple_of(start + j * LANES, LANES), LANES)
                at.block_high[level][j] = at.diag_high[:, here]
                at.block_low[level][j] = at.diag_low[:, here]
                return carry

            lax.fori_loop(0, 2 ** (level - 1), block, 0)

        def convert_last_diag():
            j = cols // LANES
            for half in range(2):
                tail = diag32[half, :, j * LANES : cols]
                tail = jnp.concatenate([tail, jnp.zeros((rows, LANES - rows), jnp.float32)], axis=1)
                mixed = jnp.where(wide_lane < rows, tail, diag32[half, :, (j - 1) * LANES : j * LANES])
                put_diag(half, pl.ds(j * LANES, LANES), pltpu.roll(mixed, rows, 1))

        def convert_off(first, last):
            def block(p, carry):
                value_high, value_low = split(off32[p])
                at.off_high[p] = value_high
                at.off_low[p] = value_low
                return carry

            lax.fori_loop(first, last, block, 0)

        arrived("diag0")
        for half in range(2):
            first = jnp.where(wide_lane < rows, diag32[half, :, 0:LANES], 0.0)
            put_diag(half, pl.ds(0, LANES), first if half == 0 else pltpu.roll(first, rows, 1))
        convert_diag(1, low_cols // LANES)
        arrived("off0")
        convert_off(0, low_pairs)
        received("tiles", at.tiles_v.at[1 - core])
        to_smem = pltpu.make_async_copy(at.tiles_v, at.tiles_s, local_sem.at[4])
        to_smem.start()
        to_smem.wait()
        tiles = at.tiles_s

        received("side", at.side_in.at[pl.ds(0, slots - 1)])
        turned = []
        for s in range(slots):
            value = unfold(at.side_in[s])
            turned.append(pltpu.roll(value, s * chunk, 1) if s else value)
        for level in range(levels):
            value = turned[0]
            for s in range(1, slots):
                value = jnp.where(lane_block == (s + level) % slots, turned[s], value)
            at.b[level] = pltpu.roll(value, LANES - level * chunk, 1) if level else value

        def diag_block(level):
            if level == 0:
                place = pl.ds(0, LANES)
            else:
                place = pl.ds(rows * 2**level, rows * 2**level)
            return at.diag_high[:, place], at.diag_low[:, place]

        def contribute(source, level):
            p = pair_slot(source, level)
            known = at.y[source]
            stacked = jnp.concatenate([jnp.where(left_half, known, 0.0), jnp.where(left_half, 0.0, known)], axis=0)
            out = product(stacked, at.off_high[p], at.off_low[p], NN)
            pieces = []
            for half in range(2):
                for t in range(2):
                    piece = out[half * group : (half + 1) * group, t * LANES : (t + 1) * LANES]
                    pieces.append((piece, tiles[half, t, p]))
            acc = at.acc[level]
            count = 2 ** (level - 1)

            def add(target, carry):
                value = acc[target]
                for piece, number in pieces:
                    value = value - piece * (number == target).astype(jnp.float32)
                acc[target] = value
                return carry

            if count <= 4:
                for target in range(count):
                    add(target, 0)
            else:
                lax.fori_loop(0, count, add, 0)

        def gather_known(ancestor, level):
            p = pair_slot(level, ancestor)
            full = at.full[ancestor]
            halves = []
            for half in range(2):
                halves.append(jnp.concatenate([full[tiles[half, t, p]] for t in range(2)], axis=1))
            out = product(jnp.concatenate(halves, axis=0), at.off_high[p], at.off_low[p], NT)
            at.w[level] += jnp.where(left_half, out[:group], out[group:])

        def broadcast(name, source, level):
            count = 2 ** (level - 1)
            place = lax.rem(chip, count)
            target = table[name]

            def one(step, carry):
                _, device = plane_peer(count, step)
                send(name, source, target.at[place], device)
                return carry

            lax.fori_loop(0, count - 1, one, 0)

        def scatter(name, source, level):
            count = 2 ** (level - 1)
            place = lax.rem(chip, count)
            target = table[name]

            def one(step, carry):
                index, device = plane_peer(count, step)
                send(name, source.at[index], target.at[place], device)
                return carry

            lax.fori_loop(0, count - 1, one, 0)

        def await_all(name, level):
            count = 2 ** (level - 1)
            received(name, table[name].at[pl.ds(0, count - 1)])

        def total(ref, count):
            value = ref[0]
            for place in range(1, count):
                value = value + ref[place]
            return value

        def build_mix(level):
            count = 2 ** (level - 1)
            first_chip = in_group - lax.rem(chip, count)
            p = pair_slot(level - 1, level)
            rows_of, mix, numbers = at.lrow[level], at.mix[level], at.ptiles_s
            block_high, block_low = at.block_high[level], at.block_low[level]
            copy_blocks(level)

            def one(index, carry):
                value = rows_of[index]
                high_part = value.astype(jnp.bfloat16).astype(jnp.float32)
                both = jnp.concatenate([high_part, value - high_part], axis=0).astype(jnp.bfloat16)
                out = jnp.zeros((2 * chunk, LANES), jnp.float32)
                rest = jnp.zeros((2 * chunk, LANES), jnp.float32)
                for t in range(2):
                    number = numbers[first_chip + index, t, p]
                    piece = both[:, t * LANES : (t + 1) * LANES]
                    out += lax.dot_general(piece, block_high[number], NT, preferred_element_type=jnp.float32)
                    rest += lax.dot_general(piece, block_low[number], NT, preferred_element_type=jnp.float32)
                mix[index, own_rows] = out[:chunk] + out[chunk:] + rest[:chunk]
                return carry

            lax.fori_loop(0, count, one, 0)

            def give(step, carry):
                their_z = lax.rem(z + grid + (1 - 2 * core) * outward(step, grid), grid)
                part = mix.at[:, own_rows]
                send(("mix", level), part, part, (leaf, their_z))
                return carry

            lax.fori_loop(0, grid - 1, give, 0)

        def swap_mix(level):
            mix = at.mix[level]
            received(("mix", level), mix.at[:, pl.ds(0, grid - 1)])
            half = mix.at[:, pl.ds(core * grid, grid)]
            send(("swap", level), half, half, partner)

        def finish_mix(level):
            count = 2 ** (level - 1)
            mix = at.mix[level]
            received(("swap", level), mix.at[:, pl.ds((1 - core) * grid, grid)])

            def one(index, carry):
                value_high, value_low = split(mix[index].reshape(LANES, LANES))
                spot = pl.ds(pl.multiple_of(index * LANES, LANES), LANES)
                at.mix_high[level][spot, :] = value_high
                at.mix_low[level][spot, :] = value_low
                return carry

            lax.fori_loop(0, count, one, 0)

        at.y[0] = product(at.b[0], *diag_block(0), NT)
        contribute(0, 1)
        at.y[1] = product(at.b[1] + at.acc[1][0], *diag_block(1), NT)
        contribute(0, 2)
        def start_sums(level):
            count = 2 ** (level - 1)
            place = lax.rem(chip, count)
            acc, up = at.acc[level], at.up[level]
            if level <= ONE_STEP:
                acc[place] += at.b[level]
                broadcast(("up", level), acc, level)
                up[place] = acc[...]
            else:
                scatter(("up", level), acc, level)
                up[place] = acc[place]

        def spread_sum(level):
            count = 2 ** (level - 1)
            place = lax.rem(chip, count)
            await_all(("up", level), level)
            summed = at.sum[level]
            summed[place] = at.b[level] + total(at.up[level], count)
            broadcast(("sum", level), summed.at[place], level)

        def side_by_side(value, count):
            return jnp.concatenate([value[t] for t in range(count)], axis=1)

        def solve_level(level):
            count = 2 ** (level - 1)
            if level <= ONE_STEP:
                await_all(("up", level), level)
                whole = total(at.up[level], count)
            else:
                await_all(("sum", level), level)
                whole = at.sum[level][...]
            return product(side_by_side(whole, count), *diag_block(level), NT)

        contribute(1, 2)
        start_sums(2)
        contribute(0, 3)
        contribute(1, 3)
        arrived("off1")
        convert_off(low_pairs, pairs)
        at.y[2] = solve_level(2)
        contribute(2, 3)
        start_sums(3)
        for source in range(3):
            contribute(source, 4)
        arrived("diag1")
        convert_diag(low_cols // LANES, rows * 2 ** (MIX_TOP + 1) // LANES)
        received("ptiles", at.ptiles_v.at[pl.ds(0, group_chips - 1)])
        for upper in range(ONE_STEP + 1, MIX_TOP + 1):
            await_all(("lrow", upper), upper)
        numbers = pltpu.make_async_copy(at.ptiles_v, at.ptiles_s, local_sem.at[7])
        numbers.start()
        numbers.wait()
        build_mix(MIX_TOP)
        at.y[3] = solve_level(3)
        contribute(3, 4)
        start_sums(4)
        for source in range(4):
            contribute(source, MIX_TOP)
        start_sums(MIX_TOP)
        spread_sum(4)
        build_mix(4)
        spread_sum(MIX_TOP)
        at.y[4] = solve_level(4)
        count = 2 ** (MIX_TOP - 1)
        new = at.new[MIX_TOP]
        place = lax.rem(chip, count)
        new[place] = at.y[4]
        broadcast(("new", MIX_TOP), new.at[place], MIX_TOP)
        swap_mix(MIX_TOP)
        known = solve_level(MIX_TOP)
        for source in range(MIX_TOP):
            contribute(source, top)
        finish_mix(MIX_TOP)
        await_all(("new", MIX_TOP), MIX_TOP)
        at.y[MIX_TOP] = known - product(
            side_by_side(new[...], count), at.mix_high[MIX_TOP][...], at.mix_low[MIX_TOP][...], NN
        )
        contribute(MIX_TOP, top)
        start_sums(top)
        convert_diag(rows * 2**top // LANES, cols // LANES)
        convert_last_diag()
        spread_sum(top)
        swap_mix(4)
        finish_mix(4)
        at.y[top] = solve_level(top)

        def pack(values, name, outbox, inbox):
            turned = []
            for level in range(levels):
                value = values[level]
                turned.append(pltpu.roll(value, level * chunk, 1) if level else value)
            for s in range(slots):
                value = turned[0]
                for level in range(1, levels):
                    value = jnp.where(lane_block == (s + level) % slots, turned[level], value)
                outbox[s] = fold(pltpu.roll(value, LANES - s * chunk, 1) if s else value)

            def one(step, carry):
                index, device = row_peer(step)
                send(name, outbox.at[index], inbox.at[own_rhs], device)
                return carry

            lax.fori_loop(0, slots - 1, one, 0)
            inbox[own_rhs] = outbox[own_rows]

        def unpack(name, inbox, target):
            received(name, inbox.at[pl.ds(0, slots - 1)])
            value = unfold(inbox[...]).reshape(slots * group, LANES).T
            for level in range(levels):
                target[level] = value[level * chunk : (level + 1) * chunk]

        def start_level(level):
            count = 2 ** (level - 1)
            place = lax.rem(chip, count)
            residue = at.y[level] - at.w[level]
            part, down = at.part[level], at.down[level]
            value = product(residue, *diag_block(level), NN)
            for t in range(count):
                part[t] = value[:, t * LANES : (t + 1) * LANES]
            if level <= ONE_STEP:
                broadcast(("down", level), part, level)
                down[place] = part[...]
                return
            if level > MIX_TOP:
                scatter(("down", level), part, level)
                down[place] = part[place]
                return
            mpart, mid = at.mpart[level], at.mid[level]
            value = product(residue, at.mix_high[level][...], at.mix_low[level][...], NT)
            for t in range(count):
                mpart[t] = value[:, t * LANES : (t + 1) * LANES]
            scatter(("mid", level), mpart, level)
            mid[place] = mpart[place]
            scatter(("down", level), part, level)
            down[place] = part[place]

        def spread_x(level):
            count = 2 ** (level - 1)
            place = lax.rem(chip, count)
            await_all(("down", level), level)
            value = total(at.down[level], count)
            at.x[level] = value
            at.full[level][place] = value
            broadcast(("full", level), at.full[level].at[place], level)

        def through_mix(level):
            await_all(("mid", level), level)
            at.w[level - 1] += total(at.mid[level], 2 ** (level - 1))

        def whole_x(level):
            count = 2 ** (level - 1)
            await_all(("down", level), level)
            at.full[level][...] = total(at.down[level], count)
            at.x[level] = at.full[level][lax.rem(chip, count)]

        start_level(top)
        pack(at.y, "fwd", at.fwd_out, at.fwd_in)
        spread_x(top)
        await_all(("full", top), top)
        gather_known(top, MIX_TOP)
        start_level(MIX_TOP)
        gather_known(top, MIX_TOP - 1)
        through_mix(MIX_TOP)
        start_level(ONE_STEP + 1)
        spread_x(MIX_TOP)
        for below in range(ONE_STEP, -1, -1):
            gather_known(top, below)
        through_mix(ONE_STEP + 1)
        await_all(("full", MIX_TOP), MIX_TOP)
        gather_known(MIX_TOP, ONE_STEP)
        start_level(ONE_STEP)
        spread_x(ONE_STEP + 1)
        for below in range(ONE_STEP - 1, -1, -1):
            gather_known(ONE_STEP + 2, below)
        unpack("fwd", at.fwd_in, fwd_ref)
        whole_x(ONE_STEP)
        await_all(("full", ONE_STEP + 1), ONE_STEP + 1)
        gather_known(ONE_STEP + 1, 2)
        gather_known(ONE_STEP, 2)
        start_level(2)
        for below in (1, 0):
            gather_known(ONE_STEP + 1, below)
            gather_known(ONE_STEP, below)
        whole_x(2)
        gather_known(2, 1)
        value = product(at.y[1] - at.w[1], *diag_block(1), NN)
        at.x[1] = value
        at.full[1][0] = value
        gather_known(2, 0)
        gather_known(1, 0)
        at.x[0] = product(at.y[0] - at.w[0], *diag_block(0), NN)
        pack(at.x, "sol", at.sol_out, at.sol_in)
        unpack("sol", at.sol_in, sol_ref)
        for name, view in sent:
            await_bytes(view, send_sem.at[slot_of[name]])

    return kernel


def solution(mesh):
    grid = mesh.shape["grid"]

    def local(right_side, diag_inv, off_diag, tile_rows):
        levels, rhs, chunk = right_side.shape
        rows, cols = diag_inv.shape
        pairs = off_diag.shape[0]
        slots = 2 * grid
        group = rhs // slots
        side = jnp.transpose(right_side, (0, 2, 1))
        off = jnp.transpose(off_diag, (0, 2, 1))
        tiles = jnp.transpose(tile_rows[:, :, 0], (1, 0))
        plan, moves = scratch_plan(levels, pairs, rows, cols, group, slots)
        vmem = pl.BlockSpec(memory_space=pltpu.VMEM)
        hbm = pl.BlockSpec(memory_space=pltpu.HBM)
        out = jax.ShapeDtypeStruct(side.shape, jnp.float32)
        forward, backward = pl.pallas_call(
            make_kernel(levels, list(plan), moves, rows, cols, group, grid),
            out_shape=(out, out),
            in_specs=[hbm, hbm, hbm, hbm],
            out_specs=(vmem, vmem),
            scratch_shapes=list(plan.values()),
            compiler_params=pltpu.CompilerParams(
                collective_id=0, has_side_effects=True, vmem_limit_bytes=48 * 2**20
            ),
            name="tree_solve",
        )(*(pltpu.with_memory_space_constraint(part, pltpu.HBM) for part in (side, diag_inv, off, tiles)))
        return jnp.transpose(forward, (0, 2, 1)), jnp.transpose(backward, (0, 2, 1))

    in_specs = (
        P(None, None, ("leaf", "grid")),
        P("leaf", None),
        P(None, None, "leaf"),
        P(None, None, "leaf"),
    )
    out_specs = (P(None, None, ("leaf", "grid")), P(None, None, ("leaf", "grid")))
    return jax.shard_map(local, mesh=mesh, in_specs=in_specs, out_specs=out_specs, check_vma=False)
```
